32 devices in a mesh: sky: 2 (over x), seg: 16 (over z, y, core).
Axes of the slice: x: 2, y: 2, z: 4, core: 2. Of those that a mesh axis runs over, the one named last changes fastest.
Arguments:
- strain_series: bfloat16 [32, 2, 65536], P(('sky', 'seg')), parts along dimension 0, may hold values from -6 to 6
- antenna: float32 [32, 2, 65536], P(('sky', 'seg')), parts along dimension 0, may hold values from -160 to 160, as said below
- drift: int32 [32, 6], P(('sky', 'seg')), parts along dimension 0, may hold values from -2 to 2
- tracks: int32 [64, 16], replicated, may hold values from 0 to 5
Outputs:
- track_stat: float32 [128, 65536], P('sky', 'seg'), parts along dimension 0
The draws below stay inside these ranges and needn't reach their ends.
There are 2 independent parts, one for each index of `sky`. The reference program is written for one: setup_inputs(seed, part) draws one part's arguments, and reference() takes and returns one part's arrays. A program takes and returns all parts, laid end to end along the dimension named above; an argument that names none is the same for every part. Nothing has to cross between parts.
Inputs may be any that keep to these rules, and one draw needn't show every extreme that they name: `antenna`: row 0 holds the a weights, row 1 the b weights of each segment.
All inputs are finite; a program needn't handle non-finite values.
Results may differ from the reference program's by a relative error of at most 0.0015.
Values sent between devices are 32-bit elements; how exact they have to be, the bound alone decides.
No kernel may reach another device: no remote copies, remote signals or barrier semaphores. Data moves between devices by JAX's collectives and lax.ppermute only.
A program may use at most 192 MiB of HBM per device.

```python
import math
import jax
import jax.numpy as jnp
from jax import lax

NBIN = 65536
DFT_ROWS = 256
BLK = 128
DMAX = 2
KCOH = 6
NTRACK = 64
NSEG = 16


def draw_antenna(key, part):
    key_noise = jax.random.fold_in(key, 11)
    key_corr = jax.random.fold_in(key, 12)
    key_level = jax.random.fold_in(key, 13)
    noise = jnp.clip(jax.random.normal(key_noise, (NSEG, 2, NBIN), jnp.float32), -5.0, 5.0)
    levels = jax.random.uniform(key_level, (NSEG, 16), jnp.float32, 0.0, math.log(10.0))
    corr = jax.random.uniform(key_corr, (NSEG, 1), jnp.float32, -0.995, 0.995)
    envelope = jnp.repeat(jnp.exp(levels), NBIN // 16, axis=1)
    first = envelope * noise[:, 0]
    second = envelope * (corr * noise[:, 0] + jnp.sqrt(1.0 - corr * corr) * noise[:, 1])
    return jnp.stack([first, second], 1)


def plant(array, key, low, largest):
    longest = array.shape.index(max(array.shape))
    spots = []
    for shift in (0, 1):
        where = [jax.random.randint(jax.random.fold_in(key, axis), (), 0, length) for axis, length in enumerate(array.shape)]
        where[longest] = (where[longest] + shift) % array.shape[longest]
        spots.append(tuple(where))
    return array.at[spots[0]].set(low).at[spots[1]].set(largest)


def steps_of(stream_key, dims, shards, smallest, high):
    loudness, own = 1.0, jax.random.fold_in(stream_key, 6)
    for axis_at, shards_of in shards:
        heights = jnp.exp(jax.random.uniform(jax.random.fold_in(own, axis_at), (shards_of,), jnp.float32, smallest / len(shards), high / len(shards)))
        loudness = loudness * jnp.repeat(heights, dims[axis_at] // shards_of).reshape([-1 if axis == axis_at else 1 for axis in range(len(dims))])
    return loudness


def bell_draw(rng, dims, scale, most, cuts=(), kind=jnp.bfloat16):
    result = scale * jax.random.normal(rng, dims, jnp.float32)
    if cuts:
        result = result * steps_of(rng, dims, cuts, -0.22, 0.18)
    return jnp.clip(result, -most, most).astype(kind)


def setup_inputs(seed: int = 0, part: int = 0) -> dict:
    keys = jax.random.split(jax.random.key(seed), 5)
    part_splits = jax.random.split(jax.random.fold_in(keys[4], part), 5)
    strain_series = bell_draw(part_splits[0], (NSEG, 2, NBIN), 1.0, 6.0, ((0, 16),))
    antenna = draw_antenna(jax.random.fold_in(jax.random.fold_in(keys[4], part), 71), part)
    drift = plant(jax.random.randint(part_splits[2], (NSEG, KCOH), 0 - DMAX, DMAX + 1), jax.random.fold_in(part_splits[2], 1), 0 - DMAX, DMAX).astype(jnp.int32)
    tracks = plant(jax.random.randint(keys[3], (NTRACK, NSEG), 0, KCOH), jax.random.fold_in(keys[3], 1), 0, KCOH - 1).astype(jnp.int32)
    return {"strain_series": strain_series, "antenna": antenna, "drift": drift, "tracks": tracks}


chirp_step = 3.0
tiny_eps = 1e-6


def section_tables(points, first_rows):
    second_rows = points // first_rows
    outer_index = jnp.arange(first_rows, dtype=jnp.int32)
    inner_index = jnp.arange(second_rows, dtype=jnp.int32)
    first_angle = (2.0 * math.pi / first_rows) * ((outer_index[:, None] * outer_index[None, :]) % first_rows).astype(jnp.float32)
    cos_one, sin_one = jnp.cos(first_angle), jnp.sin(first_angle)
    left_table = jnp.stack([jnp.stack([cos_one, sin_one]), jnp.stack([-sin_one, cos_one])]).astype(jnp.bfloat16)
    second_angle = (2.0 * math.pi / second_rows) * ((inner_index[:, None] * inner_index[None, :]) % second_rows).astype(jnp.float32)
    cos_two, sin_two = jnp.cos(second_angle), jnp.sin(second_angle)
    right_table = jnp.stack([jnp.stack([cos_two, -sin_two]), jnp.stack([sin_two, cos_two])]).astype(jnp.bfloat16)
    twist_angle = (2.0 * math.pi / points) * ((outer_index[:, None] * inner_index[None, :]) % points).astype(jnp.float32)
    return left_table, right_table, jnp.cos(twist_angle), jnp.sin(twist_angle)


def coherent_stat(series, weights, left_table, right_table, twist_cos, twist_sin):
    seg_rows = series.shape[0]
    points = series.shape[2]
    first_rows = left_table.shape[2]
    second_rows = points // first_rows
    position = jnp.arange(points, dtype=jnp.float32) / points
    chirp_rate = (jnp.arange(KCOH, dtype=jnp.float32) - (KCOH - 1) / 2.0) * chirp_step
    phases = (2.0 * math.pi) * chirp_rate[:, None] * (position * position)[None, :]
    phase_cos, phase_sin = jnp.cos(phases), jnp.sin(phases)
    series_real = series[:, 0].astype(jnp.float32)[:, None, :]
    series_imag = series[:, 1].astype(jnp.float32)[:, None, :]
    demod_real = series_real * phase_cos + series_imag * phase_sin
    demod_imag = series_imag * phase_cos - series_real * phase_sin
    weight_a = weights[:, 0][:, None, :]
    weight_b = weights[:, 1][:, None, :]
    with_a = jnp.stack([weight_a * demod_real, weight_a * demod_imag], 2)
    with_b = jnp.stack([weight_b * demod_real, weight_b * demod_imag], 2)
    weighted = jnp.stack([with_a, with_b], 2).astype(jnp.bfloat16)
    weighted = weighted.reshape(seg_rows * KCOH * 2, 2, first_rows, second_rows)
    section_one = jnp.einsum('oikn,binm->bokm', left_table.astype(jnp.float32), weighted.astype(jnp.float32))
    one_real, one_imag = section_one[:, 0], section_one[:, 1]
    twisted_real = one_real * twist_cos + one_imag * twist_sin
    twisted_imag = one_imag * twist_cos - one_real * twist_sin
    middle = jnp.stack([twisted_real, twisted_imag], 1).astype(jnp.bfloat16)
    spectra = jnp.einsum('bikm,ioml->bolk', middle.astype(jnp.float32), right_table.astype(jnp.float32))
    spectra = spectra.reshape(seg_rows, KCOH, 2, 2, points)
    a_real, a_imag = spectra[:, :, 0, 0], spectra[:, :, 0, 1]
    b_real, b_imag = spectra[:, :, 1, 0], spectra[:, :, 1, 1]
    weight_aa = jnp.mean(weights[:, 0] * weights[:, 0], axis=-1) + tiny_eps
    weight_bb = jnp.mean(weights[:, 1] * weights[:, 1], axis=-1) + tiny_eps
    weight_ab = jnp.mean(weights[:, 0] * weights[:, 1], axis=-1)
    determinant = jnp.maximum(weight_aa * weight_bb - weight_ab * weight_ab, 0.1 * weight_aa * weight_bb)
    energy = (weight_bb[:, None, None] * (a_real * a_real + a_imag * a_imag)
              + weight_aa[:, None, None] * (b_real * b_real + b_imag * b_imag)
              - 2.0 * weight_ab[:, None, None] * (a_real * b_real + a_imag * b_imag))
    return energy / (points * determinant[:, None, None])


def drift_blocks(padded, offsets, extent, amount):
    summed = jnp.zeros(padded.shape[:-2] + (amount, padded.shape[-1]), padded.dtype)
    for offset in range(-extent, extent + 1):
        window = padded[..., extent - offset:extent - offset + amount, :]
        summed = summed + jnp.where((offsets == offset)[..., None, None], window, 0.0)
    return summed


def reference(strain_series, antenna, drift, tracks):
    left_table, right_table, twist_cos, twist_sin = section_tables(NBIN, DFT_ROWS)

    def one_segment(item):
        series, weights = item
        return coherent_stat(series[None], weights[None], left_table, right_table, twist_cos, twist_sin)[0]

    stats = lax.map(one_segment, (strain_series, antenna))
    blocks = stats.reshape(NSEG, KCOH, NBIN // BLK, BLK)
    padded = jnp.pad(blocks, ((0, 0), (0, 0), (DMAX, DMAX), (0, 0)))
    moved = drift_blocks(padded, drift, DMAX, NBIN // BLK).reshape(NSEG, KCOH, NBIN)
    levels = jnp.arange(KCOH, dtype=jnp.int32)
    pick = (tracks[:, :, None] == levels[None, None, :]).astype(jnp.float32)
    summed = jnp.einsum('jsk,skf->jf', pick, moved, precision=lax.Precision.HIGHEST)
    return summed / NSEG
```

```python
import functools
import math

import jax
import jax.numpy as jnp
import numpy as np
from jax import lax
from jax.experimental import pallas as pl
from jax.experimental.pallas import tpu as pltpu
from jax.sharding import PartitionSpec as P

BLK = 128
DMAX = 2
KCOH = 6
CHIRP_STEP = 3.0
TINY = 1e-06
PAD = 8
F32 = jnp.float32
BF16 = jnp.bfloat16


def dft_table(rows):
    index = np.arange(rows)
    angle = 2.0 * np.pi / rows * (index[:, None] * index[None, :] % rows)
    cos, sin = np.cos(angle), np.sin(angle)
    return jnp.asarray(np.block([[cos, sin], [-sin, cos]]), F32).astype(BF16)


def twist_table(rows):
    index = np.arange(rows)
    angle = 2.0 * np.pi / (rows * rows) * (index[:, None] * index[None, :])
    return jnp.asarray(np.stack([np.cos(angle), np.sin(angle)]), F32)


def chirp_table(rows, pairs):
    position = np.arange(rows * rows, dtype=np.float64) / (rows * rows)
    rates = (np.arange(KCOH) - (KCOH - 1) / 2.0) * CHIRP_STEP
    rates = np.array([rates[KCOH - 1 - pair] for pair in pairs])
    angle = 2.0 * np.pi * rates[:, None] * (position * position)[None, :]
    table = np.stack([np.cos(angle), np.sin(angle)], 1)
    return jnp.asarray(table.reshape(len(pairs), 2, rows, rows), F32)


def stat_kernel(
    pairs, count, drift, series, weights, table, twist, chirp, out, lanes, prep, coef, moved
):
    rows = table.shape[0] // 2
    halves = rows // BLK
    step = pl.program_id(0)
    me = lax.axis_index("seg")
    core, chip = lax.rem(me, 2), lax.div(me, 2)

    def take(ref, row):
        pieces = [
            ref[pl.ds(2 * half + row, rows, stride=2 * halves), :] for half in range(halves)
        ]
        return jnp.concatenate(pieces, axis=1)

    @pl.when(step == 0)
    def _():
        lanes[...] = series[...].astype(F32)
        real, imag = take(lanes, 0), take(lanes, 1)
        first, second = take(weights, 0), take(weights, 1)
        prep[0] = first * real
        prep[1] = first * imag
        prep[2] = second * real
        prep[3] = second * imag
        points = rows * rows
        aa = jnp.sum(first * first) / points + TINY
        bb = jnp.sum(second * second) / points + TINY
        ab = jnp.sum(first * second) / points
        det = jnp.maximum(aa * bb - ab * ab, 0.1 * aa * bb)
        scale = points * det
        coef[0] = bb / scale
        coef[1] = aa / scale
        coef[2] = 2.0 * ab / scale

    cos, sin = chirp[0, 0], chirp[0, 1]
    turn_cos, turn_sin = twist[0], twist[1]
    turned = []
    for weight in range(2):
        real, imag = prep[2 * weight], prep[2 * weight + 1]
        turned.append((real * cos, imag * sin, imag * cos, real * sin))
    pair = step * 0
    for position, value in enumerate(pairs):
        pair = jnp.where(step == position, value, pair)
    for side in range(2):
        sign = 1.0 if side == 0 else -1.0
        left = jnp.concatenate([rc + sign * iS for rc, iS, _, _ in turned], axis=1)
        right = jnp.concatenate([ic - sign * rs for _, _, ic, rs in turned], axis=1)
        weighted = jnp.concatenate([left.astype(BF16), right.astype(BF16)], axis=0)
        one = jnp.dot(table[...], weighted, preferred_element_type=F32)
        spectra = []
        for weight in range(2):
            columns = slice(weight * rows, (weight + 1) * rows)
            one_real, one_imag = one[:rows, columns], one[rows:, columns]
            middle = jnp.concatenate(
                [
                    (one_real * turn_cos + one_imag * turn_sin).astype(BF16),
                    (one_imag * turn_cos - one_real * turn_sin).astype(BF16),
                ],
                axis=1,
            )
            both = lax.dot_general(
                table[...], middle, (((1,), (1,)), ((), ())), preferred_element_type=F32
            )
            spectra += [both[:rows], both[rows:]]
        ar, ai, br, bi = spectra
        energy = (
            coef[0] * (ar * ar + ai * ai)
            + coef[1] * (br * br + bi * bi)
            - coef[2] * (ar * br + ai * bi)
        )
        amount = drift[0, KCOH - 1 - pair] if side == 0 else drift[0, pair]
        moved[PAD : PAD + PAD] = jnp.zeros((PAD, BLK), F32)
        moved[PAD + halves * rows - PAD : PAD + halves * rows] = jnp.zeros((PAD, BLK), F32)
        for half in range(halves):
            moved[pl.ds(PAD + half + amount, rows, stride=halves), :] = energy[
                :, half * BLK : (half + 1) * BLK
            ]
        per = halves * rows // count
        for dest in range(count):
            other = lax.bitwise_xor(dest % 2, core)
            away = lax.bitwise_xor(dest // 2, chip)
            out[0, other, away, side] = moved[PAD + dest * per : PAD + (dest + 1) * per]


def stat(pairs, count, drift, series, weights):
    points = series.shape[0] * BLK // 2
    rows = math.isqrt(points)
    per = points // BLK // count
    shape = (len(pairs), 2, count // 2, 2, per, BLK)
    whole = lambda shape: pl.BlockSpec(shape, lambda step: (0,) * len(shape))
    return pl.pallas_call(
        functools.partial(stat_kernel, pairs, count),
        grid=(len(pairs),),
        out_shape=jax.ShapeDtypeStruct(shape, F32),
        in_specs=[
            pl.BlockSpec(memory_space=pltpu.SMEM),
            whole(series.shape),
            whole(weights.shape),
            whole((2 * rows, 2 * rows)),
            whole((2, rows, rows)),
            pl.BlockSpec((1, 2, rows, rows), lambda step: (step, 0, 0, 0)),
        ],
        out_specs=pl.BlockSpec((1,) + shape[1:], lambda step: (step, 0, 0, 0, 0, 0)),
        scratch_shapes=[
            pltpu.VMEM(series.shape, F32),
            pltpu.VMEM((4, rows, rows), F32),
            pltpu.SMEM((3,), F32),
            pltpu.VMEM((points // BLK + 2 * PAD, BLK), F32),
        ],
        compiler_params=pltpu.CompilerParams(vmem_limit_bytes=48 * 2**20),
    )(drift, series, weights, dft_table(rows), twist_table(rows), chirp_table(rows, pairs))


def sum_kernel(height, segments, tracks, meta, *refs):
    blocks, out, gathered = refs[:-2], refs[-2], refs[-1]
    per = blocks[0].shape[0] // height
    me = lax.axis_index("seg")
    core, chip = lax.rem(me, 2), lax.div(me, 2)
    level, other, away = meta[0:1], meta[1:2], meta[2:3]
    segment = 2 * lax.bitwise_xor(away, chip) + lax.bitwise_xor(other, core)
    places = lax.broadcasted_iota(jnp.int32, (segments, meta.shape[1]), 0)
    chosen = (places == segment).astype(F32).astype(BF16)
    named = jnp.dot(
        tracks[...].astype(F32).astype(BF16), chosen, preferred_element_type=F32
    )
    pick = jnp.where((named == level.astype(F32)) | (level < 0), 1.0, 0.0).astype(BF16)
    for column in range(per):
        for index, block in enumerate(blocks):
            gathered[index * height : (index + 1) * height, column * BLK : (column + 1) * BLK] = (
                block[pl.ds(column, height, stride=per), :]
            )
    for column in range(0, per * BLK, 512):
        width = min(512, per * BLK - column)
        value = gathered[:, column : column + width]
        high = value.astype(BF16)
        low = (value - high.astype(F32)).astype(BF16)
        total = jnp.dot(pick, high, preferred_element_type=F32)
        total = total + jnp.dot(pick, low, preferred_element_type=F32)
        out[:, column : column + width] = total * (1.0 / segments)


def track_sum(tracks, levels, blocks):
    height = len(levels)
    ntrack, segments = tracks.shape
    per = blocks[0].shape[0] // height
    meta = np.array(
        [
            [level, other, away]
            for away in range(len(blocks))
            for level, other in levels
        ]
    ).T
    return pl.pallas_call(
        functools.partial(sum_kernel, height, segments),
        out_shape=jax.ShapeDtypeStruct((ntrack, per * BLK), F32),
        scratch_shapes=[pltpu.VMEM((len(blocks) * height, per * BLK), F32)],
        compiler_params=pltpu.CompilerParams(vmem_limit_bytes=48 * 2**20),
    )(tracks, jnp.asarray(meta, jnp.int32), *blocks)


def local(count, strain_series, antenna, drift, tracks):
    points = strain_series.shape[2]
    tile = lambda array: array.reshape(2, points // BLK, BLK).transpose(1, 0, 2).reshape(-1, BLK)
    series, weights = tile(strain_series), tile(antenna)
    pairs = tuple(range(KCOH // 2))
    stats = stat(pairs, count, drift, series, weights)
    swap = lambda hop: [(device, device ^ hop) for device in range(count)]
    mine = stats[:, 0]
    got = lax.ppermute(stats[:, 1], "seg", swap(1))
    base = mine[0, :, 0] + got[0, :, 0]
    levels, rows = [(-1, 0)], [base]
    for other, part in enumerate((mine, got)):
        for pair in pairs:
            for side in range(2):
                level = pair if side else KCOH - 1 - pair
                if (pair, side) != (0, 0):
                    levels.append((level, other))
                    rows.append(part[pair, :, side] - part[0, :, 0])
    packed = jnp.stack(rows, 1)
    packed = packed.reshape(packed.shape[0], -1, BLK)
    blocks = [packed[0]]
    for away in range(1, count // 2):
        blocks.append(lax.ppermute(packed[away], "seg", swap(2 * away)))
    return track_sum(tracks, levels, blocks)


def solution(mesh):
    return jax.shard_map(
        functools.partial(local, mesh.shape["seg"]),
        mesh=mesh,
        in_specs=(
            P(("sky", "seg"), None, None),
            P(("sky", "seg"), None, None),
            P(("sky", "seg"), None),
            P(),
        ),
        out_specs=P("sky", "seg"),
        check_vma=False,
    )
```

```python
import functools
import math

import jax
import jax.numpy as jnp
import numpy as np
from jax import lax
from jax.experimental import pallas as pl
from jax.experimental.pallas import tpu as pltpu
from jax.sharding import PartitionSpec as P

BLK = 128
DMAX = 2
KCOH = 6
CHIRP_STEP = 3.0
TINY = 1e-06
PAD = 8
F32 = jnp.float32
BF16 = jnp.bfloat16


def dft_table(rows):
    index = np.arange(rows)
    angle = 2.0 * np.pi / rows * (index[:, None] * index[None, :] % rows)
    cos, sin = np.cos(angle), np.sin(angle)
    return jnp.asarray(np.block([[cos, sin], [-sin, cos]]), F32).astype(BF16)


def twist_table(rows):
    index = np.arange(rows)
    angle = 2.0 * np.pi / (rows * rows) * (index[:, None] * index[None, :])
    return jnp.asarray(np.stack([np.cos(angle), np.sin(angle)]), F32)


def chirp_table(rows, pairs):
    position = np.arange(rows * rows, dtype=np.float64) / (rows * rows)
    rates = (np.arange(KCOH) - (KCOH - 1) / 2.0) * CHIRP_STEP
    rates = np.array([rates[KCOH - 1 - pair] for pair in pairs])
    angle = 2.0 * np.pi * rates[:, None] * (position * position)[None, :]
    table = np.stack([np.cos(angle), np.sin(angle)], 1)
    return jnp.asarray(table.reshape(len(pairs), 2, rows, rows), F32)


def split_segment(weights, lanes, prep, coef):
    rows = prep.shape[1]
    halves = rows // BLK

    def take(ref, row):
        pieces = [
            ref[pl.ds(2 * half + row, rows, stride=2 * halves), :] for half in range(halves)
        ]
        return jnp.concatenate(pieces, axis=1)

    real, imag = take(lanes, 0), take(lanes, 1)
    first, second = take(weights, 0), take(weights, 1)
    prep[0] = first * real
    prep[1] = first * imag
    prep[2] = second * real
    prep[3] = second * imag
    points = rows * rows
    aa = jnp.sum(first * first) / points + TINY
    bb = jnp.sum(second * second) / points + TINY
    ab = jnp.sum(first * second) / points
    det = jnp.maximum(aa * bb - ab * ab, 0.1 * aa * bb)
    scale = points * det
    coef[0] = bb / scale
    coef[1] = aa / scale
    coef[2] = 2.0 * ab / scale


def one_stat(pair, side, drift, chirp, table, twist, prep, coef, moved):
    rows = table.shape[0] // 2
    halves = rows // BLK
    sign = 1.0 if side == 0 else -1.0
    cos, sin = chirp[0], chirp[1] * sign
    left = jnp.concatenate([prep[2 * w] * cos + prep[2 * w + 1] * sin for w in (0, 1)], axis=1)
    right = jnp.concatenate([prep[2 * w + 1] * cos - prep[2 * w] * sin for w in (0, 1)], axis=1)
    weighted = jnp.concatenate([left.astype(BF16), right.astype(BF16)], axis=0)
    one = jnp.dot(table[...], weighted, preferred_element_type=F32)
    turn_cos, turn_sin = twist[0], twist[1]
    spectra = []
    for weight in range(2):
        columns = slice(weight * rows, (weight + 1) * rows)
        one_real, one_imag = one[:rows, columns], one[rows:, columns]
        middle = jnp.concatenate(
            [
                (one_real * turn_cos + one_imag * turn_sin).astype(BF16),
                (one_imag * turn_cos - one_real * turn_sin).astype(BF16),
            ],
            axis=1,
        )
        both = lax.dot_general(
            table[...], middle, (((1,), (1,)), ((), ())), preferred_element_type=F32
        )
        spectra += [both[:rows], both[rows:]]
    ar, ai, br, bi = spectra
    energy = (
        coef[0] * (ar * ar + ai * ai)
        + coef[1] * (br * br + bi * bi)
        - coef[2] * (ar * br + ai * bi)
    )
    amount = drift[0, level_of(pair, side)]
    moved[PAD : PAD + PAD] = jnp.zeros((PAD, BLK), F32)
    moved[PAD + halves * rows - PAD : PAD + halves * rows] = jnp.zeros((PAD, BLK), F32)
    for half in range(halves):
        moved[pl.ds(PAD + half + amount, rows, stride=halves), :] = energy[
            :, half * BLK : (half + 1) * BLK
        ]


def level_of(pair, side):
    return pair if side else KCOH - 1 - pair


def block_of(count, per, away, other):
    me = lax.axis_index("seg")
    core, chip = lax.rem(me, 2), lax.div(me, 2)
    dest = 2 * lax.bitwise_xor(chip, away) + lax.bitwise_xor(core, other)
    return pl.ds(pl.multiple_of(PAD + dest * per, math.gcd(per, PAD)), per)


EARLY = ((1, 0), (1, 1), (0, 0), (0, 1), (2, 0), (2, 1))


def fetch(pairs, sems):
    moves = [
        pltpu.make_async_copy(source, target, sems.at[index])
        for index, (source, target) in enumerate(pairs)
    ]
    for move in moves:
        move.start()
    return moves


def stat_kernel(
    kept, count, drift, series_hbm, weights_hbm, table_hbm, twist_hbm, chirp_hbm,
    own_hbm, give_hbm,
    series, weights, table, twist, chirp, lanes, prep, coef, moved, own, give, sems, out_sems,
):
    first_pair = min(pair for pair, _ in kept)
    moves = fetch(
        [
            (series_hbm, series),
            (weights_hbm, weights),
            (chirp_hbm, chirp),
            (table_hbm, table),
            (twist_hbm, twist),
        ],
        sems,
    )
    moves[0].wait()
    lanes[...] = series[...].astype(F32)
    moves[1].wait()
    split_segment(weights, lanes, prep, coef)
    for move in moves[2:]:
        move.wait()
    per = own.shape[2]
    outs = []
    for index, (pair, side) in enumerate(kept):
        at = chirp.at[pair - first_pair]
        one_stat(pair, side, drift, at, table, twist, prep, coef, moved)
        for other, (held, target) in enumerate(((give, give_hbm), (own, own_hbm))):
            for away in range(count // 2):
                held[index, away] = moved[block_of(count, per, away, 1 - other), :]
            outs.append(
                pltpu.make_async_copy(
                    held.at[index], target.at[index], out_sems.at[2 * index + other]
                )
            )
            outs[-1].start()
    for out in outs:
        out.wait()


def stat(kept, limit, cost, count, drift, series, weights):
    points = series.shape[0] * BLK // 2
    rows = math.isqrt(points)
    per = points // BLK // count
    chips = count // 2
    pairs = tuple(sorted({pair for pair, _ in kept}))
    hbm = pl.BlockSpec(memory_space=pltpu.HBM)
    smem = pl.BlockSpec(memory_space=pltpu.SMEM)
    shape = (len(kept), chips, per, BLK)
    return pl.pallas_call(
        functools.partial(stat_kernel, kept, count),
        out_shape=(jax.ShapeDtypeStruct(shape, F32),) * 2,
        in_specs=[smem] + [hbm] * 5,
        out_specs=(hbm, hbm),
        scratch_shapes=[
            pltpu.VMEM(series.shape, BF16),
            pltpu.VMEM(weights.shape, F32),
            pltpu.VMEM((2 * rows, 2 * rows), BF16),
            pltpu.VMEM((2, rows, rows), F32),
            pltpu.VMEM((len(pairs), 2, rows, rows), F32),
            pltpu.VMEM(series.shape, F32),
            pltpu.VMEM((4, rows, rows), F32),
            pltpu.SMEM((3,), F32),
            pltpu.VMEM((points // BLK + 2 * PAD, BLK), F32),
            pltpu.VMEM(shape, F32),
            pltpu.VMEM(shape, F32),
            pltpu.SemaphoreType.DMA((5,)),
            pltpu.SemaphoreType.DMA((2 * len(kept),)),
        ],
        compiler_params=pltpu.CompilerParams(vmem_limit_bytes=limit * 2**20),
        cost_estimate=pl.CostEstimate(flops=cost, bytes_accessed=3 * 2**20, transcendentals=0),
    )(drift, series, weights, dft_table(rows), twist_table(rows), chirp_table(rows, pairs))


def sum_kernel(plan, segments, has_start, tracks, meta, *refs):
    start = refs[0] if has_start else None
    blocks, out, gathered = refs[has_start:-2], refs[-2], refs[-1]
    total_rows = gathered.shape[0]
    width = gathered.shape[1]
    me = lax.axis_index("seg")
    core, chip = lax.rem(me, 2), lax.div(me, 2)
    level, other, away = meta[0:1], meta[1:2], meta[2:3]
    segment = 2 * lax.bitwise_xor(away, chip) + lax.bitwise_xor(other, core)
    places = lax.broadcasted_iota(jnp.int32, (segments, total_rows), 0)
    chosen = (places == segment).astype(F32).astype(BF16)
    named = jnp.dot(
        tracks[...].astype(F32).astype(BF16), chosen, preferred_element_type=F32
    )
    pick = jnp.where((named == level.astype(F32)) | (level < 0), 1.0, 0.0).astype(BF16)
    per = width // BLK
    for column in range(per):
        at = 0
        for block, height in zip(blocks, plan):
            gathered[at : at + height, column * BLK : (column + 1) * BLK] = block[
                pl.ds(column, height, stride=per), :
            ]
            at += height
    for column in range(0, width, 512):
        size = min(512, width - column)
        value = gathered[:, column : column + size]
        high = value.astype(BF16)
        low = (value - high.astype(F32)).astype(BF16)
        total = jnp.dot(pick, high, preferred_element_type=F32)
        total = total + jnp.dot(pick, low, preferred_element_type=F32)
        total = total * (1.0 / segments)
        if has_start:
            total = total + start[:, column : column + size]
        out[:, column : column + size] = total


def track_sum(tracks, parts, start=None):
    ntrack, segments = tracks.shape
    plan = [len(levels) for _, levels in parts]
    width = parts[0][0].shape[0] * BLK // plan[0]
    meta = np.array([row for _, levels in parts for row in levels]).T
    starts = [] if start is None else [start]
    return pl.pallas_call(
        functools.partial(sum_kernel, plan, segments, len(starts)),
        out_shape=jax.ShapeDtypeStruct((ntrack, width), F32),
        scratch_shapes=[pltpu.VMEM((sum(plan), width), F32)],
        compiler_params=pltpu.CompilerParams(vmem_limit_bytes=32 * 2**20),
    )(tracks, jnp.asarray(meta, jnp.int32), *starts, *[block for block, _ in parts])


def local(count, strain_series, antenna, drift, tracks):
    points = strain_series.shape[2]
    tile = lambda array: array.reshape(2, points // BLK, BLK).transpose(1, 0, 2).reshape(-1, BLK)
    series, weights = tile(strain_series), tile(antenna)
    chips = count // 2
    half = chips // 2
    far, near = range(half, chips), range(half)
    swap = lambda hop: [(device, device ^ hop) for device in range(count)]
    send = lambda array, hop: lax.ppermute(array, "seg", swap(hop)) if hop else array
    pack = lambda rows: jnp.stack(rows).reshape(-1, BLK)

    own, give = stat(EARLY, 58, 10**9, count, drift, series, weights)
    got = send(give, 1)
    rows, names = [own[0] + got[0]], [(-1, 0)]
    for index, (pair, side) in enumerate(EARLY[1:]):
        for other, part in enumerate((own, got)):
            rows.append(part[1 + index] - part[0])
            names.append((level_of(pair, side), other))
    blocks = {away: send(pack([row[away] for row in rows]), 2 * away) for away in range(chips)}
    parts = {
        away: (block, [(level, other, away) for level, other in names])
        for away, block in blocks.items()
    }
    first = [parts[away] for away in near]
    last = [parts[away] for away in range(chips) if away not in near]
    return track_sum(tracks, last, track_sum(tracks, first))


def solution(mesh):
    return jax.shard_map(
        functools.partial(local, mesh.shape["seg"]),
        mesh=mesh,
        in_specs=(
            P(("sky", "seg"), None, None),
            P(("sky", "seg"), None, None),
            P(("sky", "seg"), None),
            P(),
        ),
        out_specs=P("sky", "seg"),
        check_vma=False,
    )
```

```python
import functools
import math

import jax
import jax.numpy as jnp
import numpy as np
from jax import lax
from jax.experimental import pallas as pl
from jax.experimental.pallas import tpu as pltpu
from jax.sharding import PartitionSpec as P

BLK = 128
DMAX = 2
KCOH = 6
CHIRP_STEP = 3.0
TINY = 1e-06
PAD = 8
F32 = jnp.float32
BF16 = jnp.bfloat16


def dft_table(rows):
    index = np.arange(rows)
    angle = 2.0 * np.pi / rows * (index[:, None] * index[None, :] % rows)
    cos, sin = np.cos(angle), np.sin(angle)
    return jnp.asarray(np.block([[cos, sin], [-sin, cos]]), F32).astype(BF16)


def twist_table(rows):
    index = np.arange(rows)
    angle = 2.0 * np.pi / (rows * rows) * (index[:, None] * index[None, :])
    return jnp.asarray(np.stack([np.cos(angle), np.sin(angle)]), F32)


def chirp_table(rows, pairs):
    position = np.arange(rows * rows, dtype=np.float64) / (rows * rows)
    rates = (np.arange(KCOH) - (KCOH - 1) / 2.0) * CHIRP_STEP
    rates = np.array([rates[KCOH - 1 - pair] for pair in pairs])
    angle = 2.0 * np.pi * rates[:, None] * (position * position)[None, :]
    table = np.stack([np.cos(angle), np.sin(angle)], 1)
    return jnp.asarray(table.reshape(len(pairs), 2, rows, rows), F32)


def split_segment(weights, lanes, prep, coef):
    rows = prep.shape[1]
    halves = rows // BLK

    def take(ref, row):
        pieces = [
            ref[pl.ds(2 * half + row, rows, stride=2 * halves), :] for half in range(halves)
        ]
        return jnp.concatenate(pieces, axis=1)

    real, imag = take(lanes, 0), take(lanes, 1)
    first, second = take(weights, 0), take(weights, 1)
    prep[0] = first * real
    prep[1] = first * imag
    prep[2] = second * real
    prep[3] = second * imag
    points = rows * rows
    aa = jnp.sum(first * first) / points + TINY
    bb = jnp.sum(second * second) / points + TINY
    ab = jnp.sum(first * second) / points
    det = jnp.maximum(aa * bb - ab * ab, 0.1 * aa * bb)
    scale = points * det
    coef[0] = bb / scale
    coef[1] = aa / scale
    coef[2] = 2.0 * ab / scale


def one_stat(pair, side, drift, chirp, table, twist, prep, coef, moved):
    rows = table.shape[0] // 2
    halves = rows // BLK
    sign = 1.0 if side == 0 else -1.0
    cos, sin = chirp[0], chirp[1] * sign
    left = jnp.concatenate([prep[2 * w] * cos + prep[2 * w + 1] * sin for w in (0, 1)], axis=1)
    right = jnp.concatenate([prep[2 * w + 1] * cos - prep[2 * w] * sin for w in (0, 1)], axis=1)
    weighted = jnp.concatenate([left.astype(BF16), right.astype(BF16)], axis=0)
    one = jnp.dot(table[...], weighted, preferred_element_type=F32)
    turn_cos, turn_sin = twist[0], twist[1]
    spectra = []
    for weight in range(2):
        columns = slice(weight * rows, (weight + 1) * rows)
        one_real, one_imag = one[:rows, columns], one[rows:, columns]
        middle = jnp.concatenate(
            [
                (one_real * turn_cos + one_imag * turn_sin).astype(BF16),
                (one_imag * turn_cos - one_real * turn_sin).astype(BF16),
            ],
            axis=1,
        )
        both = lax.dot_general(
            table[...], middle, (((1,), (1,)), ((), ())), preferred_element_type=F32
        )
        spectra += [both[:rows], both[rows:]]
    ar, ai, br, bi = spectra
    energy = (
        coef[0] * (ar * ar + ai * ai)
        + coef[1] * (br * br + bi * bi)
        - coef[2] * (ar * br + ai * bi)
    )
    amount = drift[0, level_of(pair, side)]
    moved[PAD : PAD + PAD] = jnp.zeros((PAD, BLK), F32)
    moved[PAD + halves * rows - PAD : PAD + halves * rows] = jnp.zeros((PAD, BLK), F32)
    for half in range(halves):
        moved[pl.ds(PAD + half + amount, rows, stride=halves), :] = energy[
            :, half * BLK : (half + 1) * BLK
        ]


def level_of(pair, side):
    return pair if side else KCOH - 1 - pair


def block_of(count, per, away, other):
    me = lax.axis_index("seg")
    core, chip = lax.rem(me, 2), lax.div(me, 2)
    dest = 2 * lax.bitwise_xor(chip, away) + lax.bitwise_xor(core, other)
    return pl.ds(pl.multiple_of(PAD + dest * per, math.gcd(per, PAD)), per)


EARLY = ((1, 0), (1, 1), (0, 0), (0, 1), (2, 0), (2, 1))


def fetch(pairs, sems):
    moves = [
        pltpu.make_async_copy(source, target, sems.at[index])
        for index, (source, target) in enumerate(pairs)
    ]
    for move in moves:
        move.start()
    return moves


def stat_kernel(
    kept, count, drift_hbm, series_hbm, weights_hbm, table_hbm, twist_hbm, chirp_hbm,
    own, give,
    series, weights, table, twist, chirp, lanes, prep, coef, moved, drift, sems,
):
    first_pair = min(pair for pair, _ in kept)
    moves = fetch(
        [
            (series_hbm, series),
            (weights_hbm, weights),
            (chirp_hbm, chirp),
            (table_hbm, table),
            (twist_hbm, twist),
            (drift_hbm, drift),
        ],
        sems,
    )
    moves[0].wait()
    lanes[...] = series[...].astype(F32)
    moves[1].wait()
    split_segment(weights, lanes, prep, coef)
    for move in moves[2:]:
        move.wait()
    per = own.shape[2]
    for index, (pair, side) in enumerate(kept):
        at = chirp.at[pair - first_pair]
        one_stat(pair, side, drift, at, table, twist, prep, coef, moved)
        for away in range(count // 2):
            own[index, away] = moved[block_of(count, per, away, 0), :]
            give[index, away] = moved[block_of(count, per, away, 1), :]


def stat(kept, limit, cost, count, drift, series, weights):
    points = series.shape[0] * BLK // 2
    rows = math.isqrt(points)
    per = points // BLK // count
    chips = count // 2
    pairs = tuple(sorted({pair for pair, _ in kept}))
    inputs = (drift, series, weights, dft_table(rows), twist_table(rows), chirp_table(rows, pairs))
    hbm = pl.BlockSpec(memory_space=pltpu.HBM)
    shape = (len(kept), chips, per, BLK)
    return pl.pallas_call(
        functools.partial(stat_kernel, kept, count),
        out_shape=(jax.ShapeDtypeStruct(shape, F32),) * 2,
        in_specs=[hbm] * 6,
        out_specs=(pl.BlockSpec(memory_space=pltpu.VMEM),) * 2,
        scratch_shapes=[
            pltpu.VMEM(series.shape, BF16),
            pltpu.VMEM(weights.shape, F32),
            pltpu.VMEM((2 * rows, 2 * rows), BF16),
            pltpu.VMEM((2, rows, rows), F32),
            pltpu.VMEM((len(pairs), 2, rows, rows), F32),
            pltpu.VMEM(series.shape, F32),
            pltpu.VMEM((4, rows, rows), F32),
            pltpu.SMEM((3,), F32),
            pltpu.VMEM((points // BLK + 2 * PAD, BLK), F32),
            pltpu.SMEM(drift.shape, jnp.int32),
            pltpu.SemaphoreType.DMA((6,)),
        ],
        compiler_params=pltpu.CompilerParams(vmem_limit_bytes=int(limit * 2**20)),
        cost_estimate=pl.CostEstimate(flops=cost, bytes_accessed=3 * 2**20, transcendentals=0),
    )(*[pltpu.with_memory_space_constraint(array, pltpu.HBM) for array in inputs])


def sum_kernel(plan, segments, has_start, tracks, meta, *refs):
    start = refs[0] if has_start else None
    blocks, out, gathered = refs[has_start:-2], refs[-2], refs[-1]
    total_rows = gathered.shape[0]
    width = gathered.shape[1]
    me = lax.axis_index("seg")
    core, chip = lax.rem(me, 2), lax.div(me, 2)
    level, other, away = meta[0:1], meta[1:2], meta[2:3]
    segment = 2 * lax.bitwise_xor(away, chip) + lax.bitwise_xor(other, core)
    places = lax.broadcasted_iota(jnp.int32, (segments, total_rows), 0)
    chosen = (places == segment).astype(F32).astype(BF16)
    named = jnp.dot(
        tracks[...].astype(F32).astype(BF16), chosen, preferred_element_type=F32
    )
    pick = jnp.where((named == level.astype(F32)) | (level < 0), 1.0, 0.0).astype(BF16)
    per = width // BLK
    for column in range(per):
        at = 0
        for block, height in zip(blocks, plan):
            gathered[at : at + height, column * BLK : (column + 1) * BLK] = block[
                pl.ds(column, height, stride=per), :
            ]
            at += height
    for column in range(0, width, 512):
        size = min(512, width - column)
        value = gathered[:, column : column + size]
        high = value.astype(BF16)
        low = (value - high.astype(F32)).astype(BF16)
        total = jnp.dot(pick, high, preferred_element_type=F32)
        total = total + jnp.dot(pick, low, preferred_element_type=F32)
        total = total * (1.0 / segments)
        if has_start:
            total = total + start[:, column : column + size]
        out[:, column : column + size] = total


def track_sum(tracks, parts, start=None):
    ntrack, segments = tracks.shape
    plan = [len(levels) for _, levels in parts]
    width = parts[0][0].shape[0] * BLK // plan[0]
    meta = np.array([row for _, levels in parts for row in levels]).T
    starts = [] if start is None else [start]
    return pl.pallas_call(
        functools.partial(sum_kernel, plan, segments, len(starts)),
        out_shape=jax.ShapeDtypeStruct((ntrack, width), F32),
        scratch_shapes=[pltpu.VMEM((sum(plan), width), F32)],
        compiler_params=pltpu.CompilerParams(vmem_limit_bytes=32 * 2**20),
    )(tracks, jnp.asarray(meta, jnp.int32), *starts, *[block for block, _ in parts])


def local(count, strain_series, antenna, drift, tracks):
    points = strain_series.shape[2]
    tile = lambda array: array.reshape(2, points // BLK, BLK).transpose(1, 0, 2).reshape(-1, BLK)
    series, weights = tile(strain_series), tile(antenna)
    chips = count // 2
    half = chips // 2
    far, near = range(half, chips), range(half)
    swap = lambda hop: [(device, device ^ hop) for device in range(count)]
    send = lambda array, hop: lax.ppermute(array, "seg", swap(hop)) if hop else array
    pack = lambda rows: jnp.stack(rows).reshape(-1, BLK)

    own, give = stat(EARLY, 32, 10**9, count, drift, series, weights)
    got = send(give, 1)
    rows, names = [own[0] + got[0]], [(-1, 0)]
    for index, (pair, side) in enumerate(EARLY[1:]):
        for other, part in enumerate((own, got)):
            rows.append(part[1 + index] - part[0])
            names.append((level_of(pair, side), other))
    blocks = {away: send(pack([row[away] for row in rows]), 2 * away) for away in (0,4,2,6,5,7,3,1)}
    parts = {
        away: (block, [(level, other, away) for level, other in names])
        for away, block in blocks.items()
    }
    first = [parts[away] for away in (0,4,2,6)]
    last = [parts[away] for away in (0,4,2,6,5,7,3,1) if away not in (0,4,2,6)]
    return track_sum(tracks, last, track_sum(tracks, first))


def solution(mesh):
    return jax.shard_map(
        functools.partial(local, mesh.shape["seg"]),
        mesh=mesh,
        in_specs=(
            P(("sky", "seg"), None, None),
            P(("sky", "seg"), None, None),
            P(("sky", "seg"), None),
            P(),
        ),
        out_specs=P("sky", "seg"),
        check_vma=False,
    )
```

```python
import functools
import math

import jax
import jax.numpy as jnp
import numpy as np
from jax import lax
from jax.experimental import pallas as pl
from jax.experimental.pallas import tpu as pltpu
from jax.sharding import PartitionSpec as P

BLK = 128
DMAX = 2
KCOH = 6
CHIRP_STEP = 3.0
TINY = 1e-06
PAD = 8
CHUNK = 1024
MOVED = 2
F32 = jnp.float32
BF16 = jnp.bfloat16


def dft_table(rows):
    index = np.arange(rows)
    angle = 2.0 * np.pi / rows * (index[:, None] * index[None, :] % rows)
    cos, sin = np.cos(angle), np.sin(angle)
    return jnp.asarray(np.block([[cos, sin], [-sin, cos]]), F32).astype(BF16)


def twist_table(rows):
    index = np.arange(rows)
    angle = 2.0 * np.pi / (rows * rows) * (index[:, None] * index[None, :])
    return jnp.asarray(np.stack([np.cos(angle), np.sin(angle)]), F32)


def chirp_table(rows, pairs):
    position = np.arange(rows * rows, dtype=np.float64) / (rows * rows)
    rates = (np.arange(KCOH) - (KCOH - 1) / 2.0) * CHIRP_STEP
    rates = np.array([rates[KCOH - 1 - pair] for pair in pairs])
    angle = 2.0 * np.pi * rates[:, None] * (position * position)[None, :]
    table = np.stack([np.cos(angle), np.sin(angle)], 1)
    return jnp.asarray(table.reshape(len(pairs), 2, rows, rows), F32)


def split_segment(weights, lanes, prep, coef):
    rows = prep.shape[1]
    halves = rows // BLK

    def take(ref, row):
        pieces = [
            ref[pl.ds(2 * half + row, rows, stride=2 * halves), :] for half in range(halves)
        ]
        return jnp.concatenate(pieces, axis=1)

    real, imag = take(lanes, 0), take(lanes, 1)
    first, second = take(weights, 0), take(weights, 1)
    prep[0] = first * real
    prep[1] = first * imag
    prep[2] = second * real
    prep[3] = second * imag
    points = rows * rows
    aa = jnp.sum(first * first) / points + TINY
    bb = jnp.sum(second * second) / points + TINY
    ab = jnp.sum(first * second) / points
    det = jnp.maximum(aa * bb - ab * ab, 0.1 * aa * bb)
    scale = points * det
    coef[0] = bb / scale
    coef[1] = aa / scale
    coef[2] = 2.0 * ab / scale


def shifted(both, amount, coef, moved):
    rows = both[0].shape[1]
    halves = rows // BLK
    ar, ai = both[0][:rows], both[0][rows:]
    br, bi = both[1][:rows], both[1][rows:]
    energy = (
        coef[0] * (ar * ar + ai * ai)
        + coef[1] * (br * br + bi * bi)
        - coef[2] * (ar * br + ai * bi)
    )
    moved[PAD : PAD + PAD] = jnp.zeros((PAD, BLK), F32)
    moved[PAD + halves * rows - PAD : PAD + halves * rows] = jnp.zeros((PAD, BLK), F32)
    for half in range(halves):
        moved[pl.ds(PAD + half + amount, rows, stride=halves), :] = energy[
            :, half * BLK : (half + 1) * BLK
        ]


def level_of(pair, side):
    return pair if side else KCOH - 1 - pair


def block_of(count, per, away, other):
    me = lax.axis_index("seg")
    core, chip = lax.rem(me, 2), lax.div(me, 2)
    dest = 2 * lax.bitwise_xor(chip, away) + lax.bitwise_xor(core, other)
    return pl.ds(pl.multiple_of(PAD + dest * per, math.gcd(per, PAD)), per)


EARLY = ((1, 0), (1, 1), (0, 0), (0, 1), (2, 0), (2, 1))


def fetch(pairs, sems):
    moves = [
        pltpu.make_async_copy(source, target, sems.at[index])
        for index, (source, target) in enumerate(pairs)
    ]
    for move in moves:
        move.start()
    return moves


def stat_kernel(
    kept, count, drift_hbm, series_hbm, weights_hbm, table_hbm, twist_hbm, chirp_hbm,
    own, give,
    series, weights, table, twist, chirp, lanes, prep, coef, moved, drift, sems,
):
    first_pair = min(pair for pair, _ in kept)
    moves = fetch(
        [
            (series_hbm, series),
            (weights_hbm, weights),
            (chirp_hbm, chirp),
            (table_hbm, table),
            (twist_hbm, twist),
            (drift_hbm, drift),
        ],
        sems,
    )
    moves[0].wait()
    lanes[...] = series[...].astype(F32)
    moves[1].wait()
    split_segment(weights, lanes, prep, coef)
    for move in moves[2:]:
        move.wait()
    per = own.shape[2]
    ones, spectra = {}, {}

    def first_step(index, weight):
        pair, side = kept[index]
        cos, sin = chirp[pair - first_pair, 0], chirp[pair - first_pair, 1]
        real, imag = prep[2 * weight], prep[2 * weight + 1]
        rc, iS, ic, rs = real * cos, imag * sin, imag * cos, real * sin
        left, right = (rc + iS, ic - rs) if side == 0 else (rc - iS, ic + rs)
        both = jnp.concatenate([left.astype(BF16), right.astype(BF16)], axis=0)
        ones[index, weight] = jnp.dot(table[...], both, preferred_element_type=F32)

    def third_step(index, weight):
        one = ones.pop((index, weight))
        rows = one.shape[0] // 2
        turn_cos, turn_sin = twist[0], twist[1]
        one_real, one_imag = one[:rows], one[rows:]
        middle = jnp.concatenate(
            [
                (one_real * turn_cos + one_imag * turn_sin).astype(BF16),
                (one_imag * turn_cos - one_real * turn_sin).astype(BF16),
            ],
            axis=1,
        )
        spectra[index, weight] = lax.dot_general(
            table[...], middle, (((1,), (1,)), ((), ())), preferred_element_type=F32
        )

    def fourth_step(index):
        held = moved.at[index % MOVED]
        both = [spectra.pop((index, weight)) for weight in range(2)]
        shifted(both, drift[0, level_of(*kept[index])], coef, held)
        for away in range(count // 2):
            own[index, away] = held[block_of(count, per, away, 0), :]
            give[index, away] = held[block_of(count, per, away, 1), :]

    for index in range(len(kept) + 1):
        for weight in range(2):
            if index < len(kept):
                first_step(index, weight)
            if index:
                third_step(index - 1, weight)
        if index:
            fourth_step(index - 1)


def stat(kept, limit, cost, count, drift, series, weights):
    points = series.shape[0] * BLK // 2
    rows = math.isqrt(points)
    per = points // BLK // count
    chips = count // 2
    pairs = tuple(sorted({pair for pair, _ in kept}))
    inputs = (drift, series, weights, dft_table(rows), twist_table(rows), chirp_table(rows, pairs))
    hbm = pl.BlockSpec(memory_space=pltpu.HBM)
    shape = (len(kept), chips, per, BLK)
    return pl.pallas_call(
        functools.partial(stat_kernel, kept, count),
        out_shape=(jax.ShapeDtypeStruct(shape, F32),) * 2,
        in_specs=[hbm] * 6,
        out_specs=(pl.BlockSpec(memory_space=pltpu.VMEM),) * 2,
        scratch_shapes=[
            pltpu.VMEM(series.shape, BF16),
            pltpu.VMEM(weights.shape, F32),
            pltpu.VMEM((2 * rows, 2 * rows), BF16),
            pltpu.VMEM((2, rows, rows), F32),
            pltpu.VMEM((len(pairs), 2, rows, rows), F32),
            pltpu.VMEM(series.shape, F32),
            pltpu.VMEM((4, rows, rows), F32),
            pltpu.SMEM((3,), F32),
            pltpu.VMEM((MOVED, points // BLK + 2 * PAD, BLK), F32),
            pltpu.SMEM(drift.shape, jnp.int32),
            pltpu.SemaphoreType.DMA((6,)),
        ],
        compiler_params=pltpu.CompilerParams(vmem_limit_bytes=int(limit * 2**20)),
        cost_estimate=pl.CostEstimate(flops=cost, bytes_accessed=3 * 2**20, transcendentals=0),
    )(*[pltpu.with_memory_space_constraint(array, pltpu.HBM) for array in inputs])


def sum_kernel(plan, segments, has_start, tracks, meta, *refs):
    start = refs[0] if has_start else None
    blocks, (out, gathered, total, sems) = refs[has_start:-4], refs[-4:]
    total_rows = gathered.shape[0]
    width = gathered.shape[1]
    me = lax.axis_index("seg")
    core, chip = lax.rem(me, 2), lax.div(me, 2)
    level, other, away = meta[0:1], meta[1:2], meta[2:3]
    segment = 2 * lax.bitwise_xor(away, chip) + lax.bitwise_xor(other, core)
    places = lax.broadcasted_iota(jnp.int32, (segments, total_rows), 0)
    chosen = (places == segment).astype(F32).astype(BF16)
    named = jnp.dot(
        tracks[...].astype(F32).astype(BF16), chosen, preferred_element_type=F32
    )
    pick = jnp.where((named == level.astype(F32)) | (level < 0), 1.0, 0.0).astype(BF16)
    per = width // BLK
    size = min(CHUNK, width)
    leave = []
    for column in range(0, width, size):
        here = slice(column, column + size)
        for tile in range(column // BLK, (column + size) // BLK):
            at = 0
            for block, height in zip(blocks, plan):
                gathered[at : at + height, tile * BLK : (tile + 1) * BLK] = block[
                    pl.ds(tile, height, stride=per), :
                ]
                at += height
        value = gathered[:, here]
        high = value.astype(BF16)
        low = (value - high.astype(F32)).astype(BF16)
        result = jnp.dot(pick, high, preferred_element_type=F32)
        result = result + jnp.dot(pick, low, preferred_element_type=F32)
        result = result * (1.0 / segments)
        if has_start:
            total[:, here] = result + start[:, here]
            leave.append(
                pltpu.make_async_copy(
                    total.at[:, here], out.at[:, here], sems.at[column // size]
                )
            )
            leave[-1].start()
        else:
            out[:, here] = result
    for move in leave:
        move.wait()


def track_sum(tracks, parts, start=None):
    ntrack, segments = tracks.shape
    plan = [len(levels) for _, levels in parts]
    width = parts[0][0].shape[0] * BLK // plan[0]
    meta = np.array([row for _, levels in parts for row in levels]).T
    starts = [] if start is None else [start]
    held = (ntrack, width) if starts else (8, BLK)
    place = pltpu.HBM if starts else pltpu.VMEM
    return pl.pallas_call(
        functools.partial(sum_kernel, plan, segments, len(starts)),
        out_shape=jax.ShapeDtypeStruct((ntrack, width), F32),
        out_specs=pl.BlockSpec(memory_space=place),
        scratch_shapes=[
            pltpu.VMEM((sum(plan), width), F32),
            pltpu.VMEM(held, F32),
            pltpu.SemaphoreType.DMA((max(1, width // CHUNK),)),
        ],
        compiler_params=pltpu.CompilerParams(vmem_limit_bytes=32 * 2**20),
    )(tracks, jnp.asarray(meta, jnp.int32), *starts, *[block for block, _ in parts])


def local(count, strain_series, antenna, drift, tracks):
    points = strain_series.shape[2]
    tile = lambda array: array.reshape(2, points // BLK, BLK).transpose(1, 0, 2).reshape(-1, BLK)
    series, weights = tile(strain_series), tile(antenna)
    chips = count // 2
    half = chips // 2
    far, near = range(half, chips), range(half)
    swap = lambda hop: [(device, device ^ hop) for device in range(count)]
    send = lambda array, hop: lax.ppermute(array, "seg", swap(hop)) if hop else array
    pack = lambda rows: jnp.stack(rows).reshape(-1, BLK)

    own, give = stat(EARLY, 32, 10**9, count, drift, series, weights)
    got = send(give, 1)
    rows, names = [own[0] + got[0]], [(-1, 0)]
    for index, (pair, side) in enumerate(EARLY[1:]):
        for other, part in enumerate((own, got)):
            rows.append(part[1 + index] - part[0])
            names.append((level_of(pair, side), other))
    blocks = {away: send(pack([row[away] for row in rows]), 2 * away) for away in (0,4,2,6,5,7,3,1)}
    parts = {
        away: (block, [(level, other, away) for level, other in names])
        for away, block in blocks.items()
    }
    first = [parts[away] for away in (0,4,2,6)]
    last = [parts[away] for away in (0,4,2,6,5,7,3,1) if away not in (0,4,2,6)]
    return track_sum(tracks, last, track_sum(tracks, first))


def solution(mesh):
    return jax.shard_map(
        functools.partial(local, mesh.shape["seg"]),
        mesh=mesh,
        in_specs=(
            P(("sky", "seg"), None, None),
            P(("sky", "seg"), None, None),
            P(("sky", "seg"), None),
            P(),
        ),
        out_specs=P("sky", "seg"),
        check_vma=False,
    )
```

```python
import functools
import math

import jax
import jax.numpy as jnp
import numpy as np
from jax import lax
from jax.experimental import pallas as pl
from jax.experimental.pallas import tpu as pltpu
from jax.sharding import PartitionSpec as P

BLK = 128
DMAX = 2
KCOH = 6
CHIRP_STEP = 3.0
TINY = 1e-06
PAD = 8
CHUNK = 1024
MOVED = 2
F32 = jnp.float32
BF16 = jnp.bfloat16


def dft_table(rows):
    index = np.arange(rows)
    angle = 2.0 * np.pi / rows * (index[:, None] * index[None, :] % rows)
    cos, sin = np.cos(angle), np.sin(angle)
    return jnp.asarray(np.block([[cos, sin], [-sin, cos]]), F32).astype(BF16)


def twist_table(rows):
    index = np.arange(rows)
    angle = 2.0 * np.pi / (rows * rows) * (index[:, None] * index[None, :])
    return jnp.asarray(np.stack([np.cos(angle), np.sin(angle)]), F32)


def chirp_table(rows, pairs):
    position = np.arange(rows * rows, dtype=np.float64) / (rows * rows)
    rates = (np.arange(KCOH) - (KCOH - 1) / 2.0) * CHIRP_STEP
    rates = np.array([rates[KCOH - 1 - pair] for pair in pairs])
    angle = 2.0 * np.pi * rates[:, None] * (position * position)[None, :]
    table = np.stack([np.cos(angle), np.sin(angle)], 1)
    return jnp.asarray(table.reshape(len(pairs), 2, rows, rows), F32)


def split_segment(weights, lanes, prep, coef):
    rows = prep.shape[1]
    halves = rows // BLK

    def take(ref, row):
        pieces = [
            ref[pl.ds(2 * half + row, rows, stride=2 * halves), :] for half in range(halves)
        ]
        return jnp.concatenate(pieces, axis=1)

    real, imag = take(lanes, 0), take(lanes, 1)
    first, second = take(weights, 0), take(weights, 1)
    prep[0] = first * real
    prep[1] = first * imag
    prep[2] = second * real
    prep[3] = second * imag
    points = rows * rows
    aa = jnp.sum(first * first) / points + TINY
    bb = jnp.sum(second * second) / points + TINY
    ab = jnp.sum(first * second) / points
    det = jnp.maximum(aa * bb - ab * ab, 0.1 * aa * bb)
    scale = points * det
    coef[0] = bb / scale
    coef[1] = aa / scale
    coef[2] = 2.0 * ab / scale


def shifted(both, amount, coef, moved):
    rows = both[0].shape[1]
    halves = rows // BLK
    ar, ai = both[0][:rows], both[0][rows:]
    br, bi = both[1][:rows], both[1][rows:]
    energy = (
        coef[0] * (ar * ar + ai * ai)
        + coef[1] * (br * br + bi * bi)
        - coef[2] * (ar * br + ai * bi)
    )
    moved[PAD : PAD + PAD] = jnp.zeros((PAD, BLK), F32)
    moved[PAD + halves * rows - PAD : PAD + halves * rows] = jnp.zeros((PAD, BLK), F32)
    for half in range(halves):
        moved[pl.ds(PAD + half + amount, rows, stride=halves), :] = energy[
            :, half * BLK : (half + 1) * BLK
        ]


def level_of(pair, side):
    return pair if side else KCOH - 1 - pair


def block_of(count, per, away, other):
    me = lax.axis_index("seg")
    core, chip = lax.rem(me, 2), lax.div(me, 2)
    dest = 2 * lax.bitwise_xor(chip, away) + lax.bitwise_xor(core, other)
    return pl.ds(pl.multiple_of(PAD + dest * per, math.gcd(per, PAD)), per)


EARLY = ((1, 0), (1, 1), (0, 0), (0, 1), (2, 0), (2, 1))


def fetch(pairs, sems):
    moves = [
        pltpu.make_async_copy(source, target, sems.at[index])
        for index, (source, target) in enumerate(pairs)
    ]
    for move in moves:
        move.start()
    return moves


def stat_kernel(
    kept, count, drift_hbm, series_hbm, weights_hbm, table_hbm, twist_hbm, chirp_hbm,
    own, give,
    series, weights, table, twist, chirp, lanes, prep, coef, moved, drift, sems,
):
    first_pair = min(pair for pair, _ in kept)
    moves = fetch(
        [
            (series_hbm, series),
            (weights_hbm, weights),
            (chirp_hbm, chirp),
            (table_hbm, table),
            (twist_hbm, twist),
            (drift_hbm, drift),
        ],
        sems,
    )
    moves[0].wait()
    lanes[...] = series[...].astype(F32)
    moves[1].wait()
    split_segment(weights, lanes, prep, coef)
    for move in moves[2:]:
        move.wait()
    per = own.shape[2]
    ones, spectra = {}, {}

    def first_step(index, weight):
        pair, side = kept[index]
        cos, sin = chirp[pair - first_pair, 0], chirp[pair - first_pair, 1]
        real, imag = prep[2 * weight], prep[2 * weight + 1]
        rc, iS, ic, rs = real * cos, imag * sin, imag * cos, real * sin
        left, right = (rc + iS, ic - rs) if side == 0 else (rc - iS, ic + rs)
        both = jnp.concatenate([left.astype(BF16), right.astype(BF16)], axis=0)
        ones[index, weight] = jnp.dot(table[...], both, preferred_element_type=F32)

    def third_step(index, weight):
        one = ones.pop((index, weight))
        rows = one.shape[0] // 2
        turn_cos, turn_sin = twist[0], twist[1]
        one_real, one_imag = one[:rows], one[rows:]
        middle = jnp.concatenate(
            [
                (one_real * turn_cos + one_imag * turn_sin).astype(BF16),
                (one_imag * turn_cos - one_real * turn_sin).astype(BF16),
            ],
            axis=1,
        )
        spectra[index, weight] = lax.dot_general(
            table[...], middle, (((1,), (1,)), ((), ())), preferred_element_type=F32
        )

    def fourth_step(index):
        held = moved.at[index % MOVED]
        both = [spectra.pop((index, weight)) for weight in range(2)]
        shifted(both, drift[0, level_of(*kept[index])], coef, held)
        for away in range(count // 2):
            own[index, away] = held[block_of(count, per, away, 0), :]
            give[index, away] = held[block_of(count, per, away, 1), :]

    for index in range(len(kept) + 1):
        for weight in range(2):
            if index < len(kept):
                first_step(index, weight)
            if index:
                third_step(index - 1, weight)
        if index:
            fourth_step(index - 1)


def stat(kept, limit, cost, count, drift, series, weights):
    points = series.shape[0] * BLK // 2
    rows = math.isqrt(points)
    per = points // BLK // count
    chips = count // 2
    pairs = tuple(sorted({pair for pair, _ in kept}))
    inputs = (drift, series, weights, dft_table(rows), twist_table(rows), chirp_table(rows, pairs))
    hbm = pl.BlockSpec(memory_space=pltpu.HBM)
    shape = (len(kept), chips, per, BLK)
    return pl.pallas_call(
        functools.partial(stat_kernel, kept, count),
        out_shape=(jax.ShapeDtypeStruct(shape, F32),) * 2,
        in_specs=[hbm] * 6,
        out_specs=(pl.BlockSpec(memory_space=pltpu.VMEM),) * 2,
        scratch_shapes=[
            pltpu.VMEM(series.shape, BF16),
            pltpu.VMEM(weights.shape, F32),
            pltpu.VMEM((2 * rows, 2 * rows), BF16),
            pltpu.VMEM((2, rows, rows), F32),
            pltpu.VMEM((len(pairs), 2, rows, rows), F32),
            pltpu.VMEM(series.shape, F32),
            pltpu.VMEM((4, rows, rows), F32),
            pltpu.SMEM((3,), F32),
            pltpu.VMEM((MOVED, points // BLK + 2 * PAD, BLK), F32),
            pltpu.SMEM(drift.shape, jnp.int32),
            pltpu.SemaphoreType.DMA((6,)),
        ],
        compiler_params=pltpu.CompilerParams(vmem_limit_bytes=int(limit * 2**20)),
        cost_estimate=pl.CostEstimate(flops=cost, bytes_accessed=3 * 2**20, transcendentals=0),
    )(*[pltpu.with_memory_space_constraint(array, pltpu.HBM) for array in inputs])


def sum_kernel(plan, segments, has_start, tracks, meta, *refs):
    start = refs[0] if has_start else None
    blocks, (out, gathered, total, sems) = refs[has_start:-4], refs[-4:]
    total_rows = gathered.shape[0]
    width = gathered.shape[1]
    me = lax.axis_index("seg")
    core, chip = lax.rem(me, 2), lax.div(me, 2)
    level, other, away = meta[0:1], meta[1:2], meta[2:3]
    segment = 2 * lax.bitwise_xor(away, chip) + lax.bitwise_xor(other, core)
    places = lax.broadcasted_iota(jnp.int32, (segments, total_rows), 0)
    chosen = (places == segment).astype(F32).astype(BF16)
    named = jnp.dot(
        tracks[...].astype(F32).astype(BF16), chosen, preferred_element_type=F32
    )
    pick = jnp.where((named == level.astype(F32)) | (level < 0), 1.0, 0.0).astype(BF16)
    per = width // BLK
    size = min(CHUNK, width)
    leave = []
    for column in range(0, width, size):
        here = slice(column, column + size)
        for tile in range(column // BLK, (column + size) // BLK):
            at = 0
            for block, height in zip(blocks, plan):
                gathered[at : at + height, tile * BLK : (tile + 1) * BLK] = block[
                    pl.ds(tile, height, stride=per), :
                ]
                at += height
        value = gathered[:, here]
        high = value.astype(BF16)
        low = (value - high.astype(F32)).astype(BF16)
        result = jnp.dot(pick, high, preferred_element_type=F32)
        result = result + jnp.dot(pick, low, preferred_element_type=F32)
        result = result * (1.0 / segments)
        if has_start:
            total[:, here] = result + start[:, here]
            leave.append(
                pltpu.make_async_copy(
                    total.at[:, here], out.at[:, here], sems.at[column // size]
                )
            )
            leave[-1].start()
        else:
            out[:, here] = result
    for move in leave:
        move.wait()


def track_sum(tracks, parts, start=None):
    ntrack, segments = tracks.shape
    plan = [len(levels) for _, levels in parts]
    width = parts[0][0].shape[0] * BLK // plan[0]
    meta = np.array([row for _, levels in parts for row in levels]).T
    starts = [] if start is None else [start]
    held = (ntrack, width) if starts else (8, BLK)
    place = pltpu.HBM if starts else pltpu.VMEM
    return pl.pallas_call(
        functools.partial(sum_kernel, plan, segments, len(starts)),
        out_shape=jax.ShapeDtypeStruct((ntrack, width), F32),
        out_specs=pl.BlockSpec(memory_space=place),
        scratch_shapes=[
            pltpu.VMEM((sum(plan), width), F32),
            pltpu.VMEM(held, F32),
            pltpu.SemaphoreType.DMA((max(1, width // CHUNK),)),
        ],
        compiler_params=pltpu.CompilerParams(vmem_limit_bytes=32 * 2**20),
    )(tracks, jnp.asarray(meta, jnp.int32), *starts, *[block for block, _ in parts])


def local(count, strain_series, antenna, drift, tracks):
    points = strain_series.shape[2]
    tile = lambda array: array.reshape(2, points // BLK, BLK).transpose(1, 0, 2).reshape(-1, BLK)
    series, weights = tile(strain_series), tile(antenna)
    chips = count // 2
    half = chips // 2
    even_first = lambda away: (away % 2, away)
    far, near = sorted(range(half, chips), key=even_first), sorted(range(1, half), key=even_first)
    order = [0] + far[:1] + near[:1] + far[1:] + near[:0:-1]
    early = order[: 1 + half - half // 4]
    swap = lambda hop: [(device, device ^ hop) for device in range(count)]
    send = lambda array, hop: lax.ppermute(array, "seg", swap(hop)) if hop else array
    pack = lambda rows: jnp.stack(rows).reshape(-1, BLK)

    own, give = stat(EARLY, 32, 10**9, count, drift, series, weights)
    got = send(give, 1)
    rows, names = [own[0] + got[0]], [(-1, 0)]
    for index, (pair, side) in enumerate(EARLY[1:]):
        for other, part in enumerate((own, got)):
            rows.append(part[1 + index] - part[0])
            names.append((level_of(pair, side), other))
    blocks = {away: send(pack([row[away] for row in rows]), 2 * away) for away in order}
    parts = {
        away: (block, [(level, other, away) for level, other in names])
        for away, block in blocks.items()
    }
    first = [parts[away] for away in early]
    last = [parts[away] for away in order if away not in early]
    return track_sum(tracks, last, track_sum(tracks, first))


def solution(mesh):
    return jax.shard_map(
        functools.partial(local, mesh.shape["seg"]),
        mesh=mesh,
        in_specs=(
            P(("sky", "seg"), None, None),
            P(("sky", "seg"), None, None),
            P(("sky", "seg"), None),
            P(),
        ),
        out_specs=P("sky", "seg"),
        check_vma=False,
    )
```

```python
import functools
import math

import jax
import jax.numpy as jnp
import numpy as np
from jax import lax
from jax.experimental import pallas as pl
from jax.experimental.pallas import tpu as pltpu
from jax.sharding import PartitionSpec as P

BLK = 128
DMAX = 2
KCOH = 6
CHIRP_STEP = 3.0
TINY = 1e-06
PAD = 8
CHUNK = 1024
MOVED = 2
F32 = jnp.float32
BF16 = jnp.bfloat16


def dft_table(rows):
    index = np.arange(rows)
    angle = 2.0 * np.pi / rows * (index[:, None] * index[None, :] % rows)
    cos, sin = np.cos(angle), np.sin(angle)
    return jnp.asarray(np.block([[cos, sin], [-sin, cos]]), F32).astype(BF16)


def twist_table(rows):
    index = np.arange(rows)
    angle = 2.0 * np.pi / (rows * rows) * (index[:, None] * index[None, :])
    return jnp.asarray(np.stack([np.cos(angle), np.sin(angle)]), F32)


def chirp_table(rows, pairs):
    position = np.arange(rows * rows, dtype=np.float64) / (rows * rows)
    rates = (np.arange(KCOH) - (KCOH - 1) / 2.0) * CHIRP_STEP
    rates = np.array([rates[KCOH - 1 - pair] for pair in pairs])
    angle = 2.0 * np.pi * rates[:, None] * (position * position)[None, :]
    table = np.stack([np.cos(angle), np.sin(angle)], 1)
    return jnp.asarray(table.reshape(len(pairs), 2, rows, rows), F32)


def split_segment(weights, lanes, prep, coef):
    rows = prep.shape[1]
    halves = rows // BLK

    def take(ref, row):
        pieces = [
            ref[pl.ds(2 * half + row, rows, stride=2 * halves), :] for half in range(halves)
        ]
        return jnp.concatenate(pieces, axis=1)

    real, imag = take(lanes, 0), take(lanes, 1)
    first, second = take(weights, 0), take(weights, 1)
    prep[0] = first * real
    prep[1] = first * imag
    prep[2] = second * real
    prep[3] = second * imag
    points = rows * rows
    aa = jnp.sum(first * first) / points + TINY
    bb = jnp.sum(second * second) / points + TINY
    ab = jnp.sum(first * second) / points
    det = jnp.maximum(aa * bb - ab * ab, 0.1 * aa * bb)
    scale = points * det
    coef[0] = bb / scale
    coef[1] = aa / scale
    coef[2] = 2.0 * ab / scale


def shifted(both, amount, coef, moved):
    rows = both[0].shape[1]
    halves = rows // BLK
    ar, ai = both[0][:rows], both[0][rows:]
    br, bi = both[1][:rows], both[1][rows:]
    energy = (
        coef[0] * (ar * ar + ai * ai)
        + coef[1] * (br * br + bi * bi)
        - coef[2] * (ar * br + ai * bi)
    )
    moved[PAD : PAD + PAD] = jnp.zeros((PAD, BLK), F32)
    moved[PAD + halves * rows - PAD : PAD + halves * rows] = jnp.zeros((PAD, BLK), F32)
    for half in range(halves):
        moved[pl.ds(PAD + half + amount, rows, stride=halves), :] = energy[
            :, half * BLK : (half + 1) * BLK
        ]


def level_of(pair, side):
    return pair if side else KCOH - 1 - pair


def block_of(count, per, away, other):
    me = lax.axis_index("seg")
    core, chip = lax.rem(me, 2), lax.div(me, 2)
    dest = 2 * lax.bitwise_xor(chip, away) + lax.bitwise_xor(core, other)
    return pl.ds(pl.multiple_of(PAD + dest * per, math.gcd(per, PAD)), per)


EARLY = ((1, 0), (1, 1), (0, 0), (0, 1), (2, 0), (2, 1))


def fetch(pairs, sems):
    moves = [
        pltpu.make_async_copy(source, target, sems.at[index])
        for index, (source, target) in enumerate(pairs)
    ]
    for move in moves:
        move.start()
    return moves


def stat_kernel(
    kept, direct, count, drift_hbm, series_hbm, weights_hbm, table_hbm, twist_hbm, chirp_hbm,
    own, give, both_cores,
    series, weights, table, twist, chirp, lanes, prep, coef, moved, drift, sems,
):
    first_pair = min(pair for pair, _ in kept)
    moves = fetch(
        [
            (series_hbm, series),
            (weights_hbm, weights),
            (chirp_hbm, chirp),
            (table_hbm, table),
            (twist_hbm, twist),
            (drift_hbm, drift),
        ],
        sems,
    )
    moves[0].wait()
    lanes[...] = series[...].astype(F32)
    moves[1].wait()
    split_segment(weights, lanes, prep, coef)
    for move in moves[2:]:
        move.wait()
    per = own.shape[2]
    ones, spectra = {}, {}

    def first_step(index, weight):
        pair, side = kept[index]
        cos, sin = chirp[pair - first_pair, 0], chirp[pair - first_pair, 1]
        real, imag = prep[2 * weight], prep[2 * weight + 1]
        rc, iS, ic, rs = real * cos, imag * sin, imag * cos, real * sin
        left, right = (rc + iS, ic - rs) if side == 0 else (rc - iS, ic + rs)
        both = jnp.concatenate([left.astype(BF16), right.astype(BF16)], axis=0)
        ones[index, weight] = jnp.dot(table[...], both, preferred_element_type=F32)

    def third_step(index, weight):
        one = ones.pop((index, weight))
        rows = one.shape[0] // 2
        turn_cos, turn_sin = twist[0], twist[1]
        one_real, one_imag = one[:rows], one[rows:]
        middle = jnp.concatenate(
            [
                (one_real * turn_cos + one_imag * turn_sin).astype(BF16),
                (one_imag * turn_cos - one_real * turn_sin).astype(BF16),
            ],
            axis=1,
        )
        spectra[index, weight] = lax.dot_general(
            table[...], middle, (((1,), (1,)), ((), ())), preferred_element_type=F32
        )

    def fourth_step(index):
        held = moved.at[index % MOVED]
        both = [spectra.pop((index, weight)) for weight in range(2)]
        shifted(both, drift[0, level_of(*kept[index])], coef, held)
        for other in range(2):
            value = held[block_of(count, per, direct, other), :]
            both_cores[other, index] = value - both_cores[other, 0] if index else value
        for at, away in enumerate(others_of(count, direct)):
            own[index, at] = held[block_of(count, per, away, 0), :]
            give[index, at] = held[block_of(count, per, away, 1), :]

    for index in range(len(kept) + 1):
        for weight in range(2):
            if index < len(kept):
                first_step(index, weight)
            if index:
                third_step(index - 1, weight)
        if index:
            fourth_step(index - 1)


def others_of(count, direct):
    return [away for away in range(count // 2) if away != direct]


def stat(kept, direct, limit, cost, count, drift, series, weights):
    points = series.shape[0] * BLK // 2
    rows = math.isqrt(points)
    per = points // BLK // count
    chips = count // 2
    pairs = tuple(sorted({pair for pair, _ in kept}))
    inputs = (drift, series, weights, dft_table(rows), twist_table(rows), chirp_table(rows, pairs))
    hbm = pl.BlockSpec(memory_space=pltpu.HBM)
    shapes = [(len(kept), chips - 1, per, BLK)] * 2 + [(2, len(kept), per, BLK)]
    return pl.pallas_call(
        functools.partial(stat_kernel, kept, direct, count),
        out_shape=tuple(jax.ShapeDtypeStruct(shape, F32) for shape in shapes),
        in_specs=[hbm] * 6,
        out_specs=(pl.BlockSpec(memory_space=pltpu.VMEM),) * 3,
        scratch_shapes=[
            pltpu.VMEM(series.shape, BF16),
            pltpu.VMEM(weights.shape, F32),
            pltpu.VMEM((2 * rows, 2 * rows), BF16),
            pltpu.VMEM((2, rows, rows), F32),
            pltpu.VMEM((len(pairs), 2, rows, rows), F32),
            pltpu.VMEM(series.shape, F32),
            pltpu.VMEM((4, rows, rows), F32),
            pltpu.SMEM((3,), F32),
            pltpu.VMEM((MOVED, points // BLK + 2 * PAD, BLK), F32),
            pltpu.SMEM(drift.shape, jnp.int32),
            pltpu.SemaphoreType.DMA((6,)),
        ],
        compiler_params=pltpu.CompilerParams(vmem_limit_bytes=int(limit * 2**20)),
        cost_estimate=pl.CostEstimate(flops=cost, bytes_accessed=3 * 2**20, transcendentals=0),
    )(*[pltpu.with_memory_space_constraint(array, pltpu.HBM) for array in inputs])


def sum_kernel(plan, segments, has_start, tracks, meta, *refs):
    start = refs[0] if has_start else None
    blocks, (out, gathered, total, sems) = refs[has_start:-4], refs[-4:]
    total_rows = gathered.shape[0]
    width = gathered.shape[1]
    me = lax.axis_index("seg")
    core, chip = lax.rem(me, 2), lax.div(me, 2)
    level, other, away = meta[0:1], meta[1:2], meta[2:3]
    segment = 2 * lax.bitwise_xor(away, chip) + lax.bitwise_xor(other, core)
    places = lax.broadcasted_iota(jnp.int32, (segments, total_rows), 0)
    chosen = (places == segment).astype(F32).astype(BF16)
    named = jnp.dot(
        tracks[...].astype(F32).astype(BF16), chosen, preferred_element_type=F32
    )
    pick = jnp.where((named == level.astype(F32)) | (level < 0), 1.0, 0.0).astype(BF16)
    per = width // BLK
    size = min(CHUNK, width)
    leave = []
    for column in range(0, width, size):
        here = slice(column, column + size)
        for tile in range(column // BLK, (column + size) // BLK):
            at = 0
            for block, height in zip(blocks, plan):
                gathered[at : at + height, tile * BLK : (tile + 1) * BLK] = block[
                    pl.ds(tile, height, stride=per), :
                ]
                at += height
        value = gathered[:, here]
        high = value.astype(BF16)
        low = (value - high.astype(F32)).astype(BF16)
        result = jnp.dot(pick, high, preferred_element_type=F32)
        result = result + jnp.dot(pick, low, preferred_element_type=F32)
        result = result * (1.0 / segments)
        if has_start:
            total[:, here] = result + start[:, here]
            leave.append(
                pltpu.make_async_copy(
                    total.at[:, here], out.at[:, here], sems.at[column // size]
                )
            )
            leave[-1].start()
        else:
            out[:, here] = result
    for move in leave:
        move.wait()


def track_sum(tracks, parts, start=None):
    ntrack, segments = tracks.shape
    plan = [len(levels) for _, levels in parts]
    width = parts[0][0].shape[0] * BLK // plan[0]
    meta = np.array([row for _, levels in parts for row in levels]).T
    starts = [] if start is None else [start]
    held = (ntrack, width) if starts else (8, BLK)
    place = pltpu.HBM if starts else pltpu.VMEM
    return pl.pallas_call(
        functools.partial(sum_kernel, plan, segments, len(starts)),
        out_shape=jax.ShapeDtypeStruct((ntrack, width), F32),
        out_specs=pl.BlockSpec(memory_space=place),
        scratch_shapes=[
            pltpu.VMEM((sum(plan), width), F32),
            pltpu.VMEM(held, F32),
            pltpu.SemaphoreType.DMA((max(1, width // CHUNK),)),
        ],
        compiler_params=pltpu.CompilerParams(vmem_limit_bytes=32 * 2**20),
    )(tracks, jnp.asarray(meta, jnp.int32), *starts, *[block for block, _ in parts])


def local(count, strain_series, antenna, drift, tracks):
    points = strain_series.shape[2]
    tile = lambda array: array.reshape(2, points // BLK, BLK).transpose(1, 0, 2).reshape(-1, BLK)
    series, weights = tile(strain_series), tile(antenna)
    chips = count // 2
    half = chips // 2
    even_first = lambda away: (away % 2, away)
    far, near = sorted(range(half, chips), key=even_first), list(range(1, half))
    order = [0] + far[:1] + near[:1] + far[1:] + near[:0:-1]
    early = order[: 1 + half - half // 4]
    swap = lambda hop: [(device, device ^ hop) for device in range(count)]
    send = lambda array, hop: lax.ppermute(array, "seg", swap(hop)) if hop else array
    pack = lambda rows: jnp.stack(rows).reshape(-1, BLK)

    direct = order[1]
    own, give, both_cores = stat(EARLY, direct, 32, 10**9, count, drift, series, weights)
    straight = send(both_cores, 2 * direct)
    got = send(give, 1)
    rows, names = [own[0] + got[0]], [(-1, 0)]
    for index, (pair, side) in enumerate(EARLY[1:]):
        for other, part in enumerate((own, got)):
            rows.append(part[1 + index] - part[0])
            names.append((level_of(pair, side), other))
    place = {away: at for at, away in enumerate(others_of(count, direct))}
    parts = {}
    for away in order:
        if away == direct:
            continue
        block = send(pack([row[place[away]] for row in rows]), 2 * away)
        parts[away] = [(block, [(level, other, away) for level, other in names])]
    straight, _ = lax.optimization_barrier((straight, parts[near[-1]][0][0] if near else straight))
    levels = [-1] + [level_of(pair, side) for pair, side in EARLY[1:]]
    parts[direct] = [
        (block.reshape(-1, BLK), [(level, other, direct) for level in levels])
        for other, block in enumerate((straight[0], send(straight[1], 1)))
    ]
    first = [part for away in early for part in parts[away]]
    last = [part for away in order if away not in early for part in parts[away]]
    return track_sum(tracks, last, track_sum(tracks, first))


def solution(mesh):
    return jax.shard_map(
        functools.partial(local, mesh.shape["seg"]),
        mesh=mesh,
        in_specs=(
            P(("sky", "seg"), None, None),
            P(("sky", "seg"), None, None),
            P(("sky", "seg"), None),
            P(),
        ),
        out_specs=P("sky", "seg"),
        check_vma=False,
    )
```

```python
import functools
import math

import jax
import jax.numpy as jnp
import numpy as np
from jax import lax
from jax.experimental import pallas as pl
from jax.experimental.pallas import tpu as pltpu
from jax.sharding import PartitionSpec as P

BLK = 128
DMAX = 2
KCOH = 6
CHIRP_STEP = 3.0
TINY = 1e-06
PAD = 8
CHUNK = 1024
MOVED = 2
F32 = jnp.float32
BF16 = jnp.bfloat16


def dft_table(rows):
    index = np.arange(rows)
    angle = 2.0 * np.pi / rows * (index[:, None] * index[None, :] % rows)
    cos, sin = np.cos(angle), np.sin(angle)
    return jnp.asarray(np.block([[cos, sin], [-sin, cos]]), F32).astype(BF16)


def twist_table(rows):
    index = np.arange(rows)
    angle = 2.0 * np.pi / (rows * rows) * (index[:, None] * index[None, :])
    return jnp.asarray(np.stack([np.cos(angle), np.sin(angle)]), F32)


def chirp_table(rows, pairs):
    position = np.arange(rows * rows, dtype=np.float64) / (rows * rows)
    rates = (np.arange(KCOH) - (KCOH - 1) / 2.0) * CHIRP_STEP
    rates = rates[KCOH // 2 :][:1]
    angle = 2.0 * np.pi * rates[:, None] * (position * position)[None, :]
    table = np.stack([np.cos(angle), np.sin(angle)], 1)
    return jnp.asarray(table.reshape(2, rows, rows), F32)


def split_segment(weights, lanes, prep, coef):
    rows = prep.shape[1]
    halves = rows // BLK

    def take(ref, row):
        pieces = [
            ref[pl.ds(2 * half + row, rows, stride=2 * halves), :] for half in range(halves)
        ]
        return jnp.concatenate(pieces, axis=1)

    real, imag = take(lanes, 0), take(lanes, 1)
    first, second = take(weights, 0), take(weights, 1)
    prep[0] = first * real
    prep[1] = first * imag
    prep[2] = second * real
    prep[3] = second * imag
    points = rows * rows
    aa = jnp.sum(first * first) / points + TINY
    bb = jnp.sum(second * second) / points + TINY
    ab = jnp.sum(first * second) / points
    det = jnp.maximum(aa * bb - ab * ab, 0.1 * aa * bb)
    scale = points * det
    coef[0] = bb / scale
    coef[1] = aa / scale
    coef[2] = 2.0 * ab / scale


def shifted(both, amount, coef, moved):
    rows = both[0].shape[1]
    halves = rows // BLK
    ar, ai = both[0][:rows], both[0][rows:]
    br, bi = both[1][:rows], both[1][rows:]
    energy = (
        coef[0] * (ar * ar + ai * ai)
        + coef[1] * (br * br + bi * bi)
        - coef[2] * (ar * br + ai * bi)
    )
    moved[PAD : PAD + PAD] = jnp.zeros((PAD, BLK), F32)
    moved[PAD + halves * rows - PAD : PAD + halves * rows] = jnp.zeros((PAD, BLK), F32)
    for half in range(halves):
        moved[pl.ds(PAD + half + amount, rows, stride=halves), :] = energy[
            :, half * BLK : (half + 1) * BLK
        ]


def level_of(pair, side):
    return pair if side else KCOH - 1 - pair


def block_of(count, per, away, other):
    me = lax.axis_index("seg")
    core, chip = lax.rem(me, 2), lax.div(me, 2)
    dest = 2 * lax.bitwise_xor(chip, away) + lax.bitwise_xor(core, other)
    return pl.ds(pl.multiple_of(PAD + dest * per, math.gcd(per, PAD)), per)


EARLY = ((1, 0), (1, 1), (0, 0), (0, 1), (2, 0), (2, 1))


def fetch(pairs, sems):
    moves = [
        pltpu.make_async_copy(source, target, sems.at[index])
        for index, (source, target) in enumerate(pairs)
    ]
    for move in moves:
        move.start()
    return moves


def stat_kernel(
    kept, direct, count, drift_hbm, series_hbm, weights_hbm, table_hbm, twist_hbm, chirp_hbm,
    own, give, both_cores,
    series, weights, table, twist, chirp, lanes, prep, coef, moved, drift, sems,
):
    first_pair = min(pair for pair, _ in kept)
    moves = fetch(
        [
            (series_hbm, series),
            (weights_hbm, weights),
            (chirp_hbm, chirp.at[KCOH // 2 - 1]),
            (table_hbm, table),
            (twist_hbm, twist),
            (drift_hbm, drift),
        ],
        sems,
    )
    moves[0].wait()
    lanes[...] = series[...].astype(F32)
    moves[1].wait()
    split_segment(weights, lanes, prep, coef)
    for move in moves[2:]:
        move.wait()
    last = KCOH // 2 - 1
    cos, sin = chirp[last, 0], chirp[last, 1]
    twice_cos, twice_sin = cos * cos - sin * sin, 2.0 * cos * sin
    for at in reversed(range(last)):
        cos, sin = cos * twice_cos - sin * twice_sin, sin * twice_cos + cos * twice_sin
        chirp[at, 0], chirp[at, 1] = cos, sin
    per = own.shape[2]
    ones, spectra = {}, {}

    def first_step(index, weight):
        pair, side = kept[index]
        cos, sin = chirp[pair - first_pair, 0], chirp[pair - first_pair, 1]
        real, imag = prep[2 * weight], prep[2 * weight + 1]
        rc, iS, ic, rs = real * cos, imag * sin, imag * cos, real * sin
        left, right = (rc + iS, ic - rs) if side == 0 else (rc - iS, ic + rs)
        both = jnp.concatenate([left.astype(BF16), right.astype(BF16)], axis=0)
        ones[index, weight] = jnp.dot(table[...], both, preferred_element_type=F32)

    def third_step(index, weight):
        one = ones.pop((index, weight))
        rows = one.shape[0] // 2
        turn_cos, turn_sin = twist[0], twist[1]
        one_real, one_imag = one[:rows], one[rows:]
        middle = jnp.concatenate(
            [
                (one_real * turn_cos + one_imag * turn_sin).astype(BF16),
                (one_imag * turn_cos - one_real * turn_sin).astype(BF16),
            ],
            axis=1,
        )
        spectra[index, weight] = lax.dot_general(
            table[...], middle, (((1,), (1,)), ((), ())), preferred_element_type=F32
        )

    def fourth_step(index):
        held = moved.at[index % MOVED]
        both = [spectra.pop((index, weight)) for weight in range(2)]
        shifted(both, drift[0, level_of(*kept[index])], coef, held)
        for other in range(2):
            value = held[block_of(count, per, direct, other), :]
            both_cores[other, index] = value - both_cores[other, 0] if index else value
        for at, away in enumerate(others_of(count, direct)):
            own[index, at] = held[block_of(count, per, away, 0), :]
            give[index, at] = held[block_of(count, per, away, 1), :]

    for index in range(len(kept) + 1):
        for weight in range(2):
            if index < len(kept):
                first_step(index, weight)
            if index:
                third_step(index - 1, weight)
        if index:
            fourth_step(index - 1)


def others_of(count, direct):
    return [away for away in range(count // 2) if away != direct]


def stat(kept, direct, limit, cost, count, drift, series, weights):
    points = series.shape[0] * BLK // 2
    rows = math.isqrt(points)
    per = points // BLK // count
    chips = count // 2
    pairs = tuple(sorted({pair for pair, _ in kept}))
    inputs = (drift, series, weights, dft_table(rows), twist_table(rows), chirp_table(rows, pairs))
    hbm = pl.BlockSpec(memory_space=pltpu.HBM)
    shapes = [(len(kept), chips - 1, per, BLK)] * 2 + [(2, len(kept), per, BLK)]
    return pl.pallas_call(
        functools.partial(stat_kernel, kept, direct, count),
        out_shape=tuple(jax.ShapeDtypeStruct(shape, F32) for shape in shapes),
        in_specs=[hbm] * 6,
        out_specs=(pl.BlockSpec(memory_space=pltpu.VMEM),) * 3,
        scratch_shapes=[
            pltpu.VMEM(series.shape, BF16),
            pltpu.VMEM(weights.shape, F32),
            pltpu.VMEM((2 * rows, 2 * rows), BF16),
            pltpu.VMEM((2, rows, rows), F32),
            pltpu.VMEM((len(pairs), 2, rows, rows), F32),
            pltpu.VMEM(series.shape, F32),
            pltpu.VMEM((4, rows, rows), F32),
            pltpu.SMEM((3,), F32),
            pltpu.VMEM((MOVED, points // BLK + 2 * PAD, BLK), F32),
            pltpu.SMEM(drift.shape, jnp.int32),
            pltpu.SemaphoreType.DMA((6,)),
        ],
        compiler_params=pltpu.CompilerParams(vmem_limit_bytes=int(limit * 2**20)),
        cost_estimate=pl.CostEstimate(flops=cost, bytes_accessed=3 * 2**20, transcendentals=0),
    )(*[pltpu.with_memory_space_constraint(array, pltpu.HBM) for array in inputs])


def sum_kernel(plan, segments, has_start, tracks, meta, *refs):
    start = refs[0] if has_start else None
    blocks, (out, gathered, total, sems) = refs[has_start:-4], refs[-4:]
    total_rows = gathered.shape[0]
    width = gathered.shape[1]
    me = lax.axis_index("seg")
    core, chip = lax.rem(me, 2), lax.div(me, 2)
    level, other, away = meta[0:1], meta[1:2], meta[2:3]
    segment = 2 * lax.bitwise_xor(away, chip) + lax.bitwise_xor(other, core)
    places = lax.broadcasted_iota(jnp.int32, (segments, total_rows), 0)
    chosen = (places == segment).astype(F32).astype(BF16)
    named = jnp.dot(
        tracks[...].astype(F32).astype(BF16), chosen, preferred_element_type=F32
    )
    pick = jnp.where((named == level.astype(F32)) | (level < 0), 1.0, 0.0).astype(BF16)
    per = width // BLK
    size = min(CHUNK, width)
    leave = []
    for column in range(0, width, size):
        here = slice(column, column + size)
        for tile in range(column // BLK, (column + size) // BLK):
            at = 0
            for block, height in zip(blocks, plan):
                gathered[at : at + height, tile * BLK : (tile + 1) * BLK] = block[
                    pl.ds(tile, height, stride=per), :
                ]
                at += height
        value = gathered[:, here]
        high = value.astype(BF16)
        low = (value - high.astype(F32)).astype(BF16)
        result = jnp.dot(pick, high, preferred_element_type=F32)
        result = result + jnp.dot(pick, low, preferred_element_type=F32)
        result = result * (1.0 / segments)
        if has_start:
            total[:, here] = result + start[:, here]
            leave.append(
                pltpu.make_async_copy(
                    total.at[:, here], out.at[:, here], sems.at[column // size]
                )
            )
            leave[-1].start()
        else:
            out[:, here] = result
    for move in leave:
        move.wait()


def track_sum(tracks, parts, start=None):
    ntrack, segments = tracks.shape
    plan = [len(levels) for _, levels in parts]
    width = parts[0][0].shape[0] * BLK // plan[0]
    meta = np.array([row for _, levels in parts for row in levels]).T
    starts = [] if start is None else [start]
    held = (ntrack, width) if starts else (8, BLK)
    place = pltpu.HBM if starts else pltpu.VMEM
    return pl.pallas_call(
        functools.partial(sum_kernel, plan, segments, len(starts)),
        out_shape=jax.ShapeDtypeStruct((ntrack, width), F32),
        out_specs=pl.BlockSpec(memory_space=place),
        scratch_shapes=[
            pltpu.VMEM((sum(plan), width), F32),
            pltpu.VMEM(held, F32),
            pltpu.SemaphoreType.DMA((max(1, width // CHUNK),)),
        ],
        compiler_params=pltpu.CompilerParams(vmem_limit_bytes=32 * 2**20),
    )(tracks, jnp.asarray(meta, jnp.int32), *starts, *[block for block, _ in parts])


def local(count, strain_series, antenna, drift, tracks):
    points = strain_series.shape[2]
    tile = lambda array: array.reshape(2, points // BLK, BLK).transpose(1, 0, 2).reshape(-1, BLK)
    series, weights = tile(strain_series), tile(antenna)
    chips = count // 2
    half = chips // 2
    even_first = lambda away: (away % 2, away)
    far, near = sorted(range(half, chips), key=even_first), sorted(range(1, half), key=even_first)
    order = [0] + far[:1] + near[:1] + far[1:] + near[:0:-1]
    early = order[: 1 + half - half // 4]
    swap = lambda hop: [(device, device ^ hop) for device in range(count)]
    send = lambda array, hop: lax.ppermute(array, "seg", swap(hop)) if hop else array
    pack = lambda rows: jnp.stack(rows).reshape(-1, BLK)

    direct = order[1]
    own, give, both_cores = stat(EARLY, direct, 32, 10**9, count, drift, series, weights)
    straight = send(both_cores, 2 * direct)
    got = send(give, 1)
    rows, names = [own[0] + got[0]], [(-1, 0)]
    for index, (pair, side) in enumerate(EARLY[1:]):
        for other, part in enumerate((own, got)):
            rows.append(part[1 + index] - part[0])
            names.append((level_of(pair, side), other))
    place = {away: at for at, away in enumerate(others_of(count, direct))}
    parts = {}
    for away in order:
        if away == direct:
            continue
        block = send(pack([row[place[away]] for row in rows]), 2 * away)
        parts[away] = [(block, [(level, other, away) for level, other in names])]
    straight, _ = lax.optimization_barrier((straight, parts[near[-1]][0][0] if near else straight))
    levels = [-1] + [level_of(pair, side) for pair, side in EARLY[1:]]
    parts[direct] = [
        (block.reshape(-1, BLK), [(level, other, direct) for level in levels])
        for other, block in enumerate((straight[0], send(straight[1], 1)))
    ]
    first = [part for away in early for part in parts[away]]
    last = [part for away in order if away not in early for part in parts[away]]
    return track_sum(tracks, last, track_sum(tracks, first))


def solution(mesh):
    return jax.shard_map(
        functools.partial(local, mesh.shape["seg"]),
        mesh=mesh,
        in_specs=(
            P(("sky", "seg"), None, None),
            P(("sky", "seg"), None, None),
            P(("sky", "seg"), None),
            P(),
        ),
        out_specs=P("sky", "seg"),
        check_vma=False,
    )
```

```python
import functools
import math

import jax
import jax.numpy as jnp
import numpy as np
from jax import lax
from jax.experimental import pallas as pl
from jax.experimental.pallas import tpu as pltpu
from jax.sharding import PartitionSpec as P

BLK = 128
DMAX = 2
KCOH = 6
CHIRP_STEP = 3.0
TINY = 1e-06
PAD = 8
CHUNK = 1024
MOVED = 2
F32 = jnp.float32
BF16 = jnp.bfloat16


def dft_table(rows):
    index = np.arange(rows)
    angle = 2.0 * np.pi / rows * (index[:, None] * index[None, :] % rows)
    cos, sin = np.cos(angle), np.sin(angle)
    return jnp.asarray(np.block([[cos, sin], [-sin, cos]]), F32).astype(BF16)


def twist_table(rows):
    index = np.arange(rows)
    angle = 2.0 * np.pi / (rows * rows) * (index[:, None] * index[None, :])
    return jnp.asarray(np.stack([np.cos(angle), np.sin(angle)]), F32)


def chirp_table(rows, pairs):
    position = np.arange(rows * rows, dtype=np.float64) / (rows * rows)
    rates = (np.arange(KCOH) - (KCOH - 1) / 2.0) * CHIRP_STEP
    rates = rates[KCOH // 2 :][:1]
    angle = 2.0 * np.pi * rates[:, None] * (position * position)[None, :]
    table = np.stack([np.cos(angle), np.sin(angle)], 1)
    return jnp.asarray(table.reshape(2, rows, rows), F32)


def split_segment(weights, lanes, prep, coef):
    rows = prep.shape[1]
    halves = rows // BLK

    def take(ref, row):
        pieces = [
            ref[pl.ds(2 * half + row, rows, stride=2 * halves), :] for half in range(halves)
        ]
        return jnp.concatenate(pieces, axis=1)

    real, imag = take(lanes, 0), take(lanes, 1)
    first, second = take(weights, 0), take(weights, 1)
    prep[0] = first * real
    prep[1] = first * imag
    prep[2] = second * real
    prep[3] = second * imag
    points = rows * rows
    aa = jnp.sum(first * first) / points + TINY
    bb = jnp.sum(second * second) / points + TINY
    ab = jnp.sum(first * second) / points
    det = jnp.maximum(aa * bb - ab * ab, 0.1 * aa * bb)
    scale = points * det
    coef[0] = bb / scale
    coef[1] = aa / scale
    coef[2] = 2.0 * ab / scale


def shifted(both, amount, coef, moved):
    rows = both[0].shape[1]
    halves = rows // BLK
    ar, ai = both[0][:rows], both[0][rows:]
    br, bi = both[1][:rows], both[1][rows:]
    energy = (
        coef[0] * (ar * ar + ai * ai)
        + coef[1] * (br * br + bi * bi)
        - coef[2] * (ar * br + ai * bi)
    )
    moved[PAD : PAD + PAD] = jnp.zeros((PAD, BLK), F32)
    moved[PAD + halves * rows - PAD : PAD + halves * rows] = jnp.zeros((PAD, BLK), F32)
    for half in range(halves):
        moved[pl.ds(PAD + half + amount, rows, stride=halves), :] = energy[
            :, half * BLK : (half + 1) * BLK
        ]


def level_of(pair, side):
    return pair if side else KCOH - 1 - pair


def block_of(count, per, away, other):
    me = lax.axis_index("seg")
    core, chip = lax.rem(me, 2), lax.div(me, 2)
    dest = 2 * lax.bitwise_xor(chip, away) + lax.bitwise_xor(core, other)
    return pl.ds(pl.multiple_of(PAD + dest * per, math.gcd(per, PAD)), per)


EARLY = ((1, 0), (1, 1), (0, 0), (0, 1), (2, 0), (2, 1))


def fetch(pairs, sems):
    moves = [
        pltpu.make_async_copy(source, target, sems.at[index])
        for index, (source, target) in enumerate(pairs)
    ]
    for move in moves:
        move.start()
    return moves


def stat_kernel(
    kept, direct, count, drift_hbm, series_hbm, weights_hbm, table_hbm, twist_hbm, chirp_hbm,
    own, give, both_cores,
    series, weights, table, twist, chirp, lanes, prep, coef, moved, drift, sems,
):
    first_pair = min(pair for pair, _ in kept)
    moves = fetch(
        [
            (series_hbm, series),
            (weights_hbm, weights),
            (chirp_hbm, chirp.at[KCOH // 2 - 1]),
            (table_hbm, table),
            (twist_hbm, twist),
            (drift_hbm, drift),
        ],
        sems,
    )
    moves[0].wait()
    lanes[...] = series[...].astype(F32)
    moves[1].wait()
    split_segment(weights, lanes, prep, coef)
    for move in moves[2:]:
        move.wait()
    last = KCOH // 2 - 1
    cos, sin = chirp[last, 0], chirp[last, 1]
    twice_cos, twice_sin = cos * cos - sin * sin, 2.0 * cos * sin
    for at in reversed(range(last)):
        cos, sin = cos * twice_cos - sin * twice_sin, sin * twice_cos + cos * twice_sin
        chirp[at, 0], chirp[at, 1] = cos, sin
    per = own.shape[2]
    ones, spectra = {}, {}

    def first_step(index, weight):
        pair, side = kept[index]
        cos, sin = chirp[pair - first_pair, 0], chirp[pair - first_pair, 1]
        real, imag = prep[2 * weight], prep[2 * weight + 1]
        rc, iS, ic, rs = real * cos, imag * sin, imag * cos, real * sin
        left, right = (rc + iS, ic - rs) if side == 0 else (rc - iS, ic + rs)
        both = jnp.concatenate([left.astype(BF16), right.astype(BF16)], axis=0)
        ones[index, weight] = jnp.dot(table[...], both, preferred_element_type=F32)

    def third_step(index, weight):
        one = ones.pop((index, weight))
        rows = one.shape[0] // 2
        turn_cos, turn_sin = twist[0], twist[1]
        one_real, one_imag = one[:rows], one[rows:]
        middle = jnp.concatenate(
            [
                (one_real * turn_cos + one_imag * turn_sin).astype(BF16),
                (one_imag * turn_cos - one_real * turn_sin).astype(BF16),
            ],
            axis=1,
        )
        spectra[index, weight] = lax.dot_general(
            table[...], middle, (((1,), (1,)), ((), ())), preferred_element_type=F32
        )

    def fourth_step(index):
        held = moved.at[index % MOVED]
        both = [spectra.pop((index, weight)) for weight in range(2)]
        shifted(both, drift[0, level_of(*kept[index])], coef, held)
        for other in range(2):
            value = held[block_of(count, per, direct, other), :]
            both_cores[other, index] = value - both_cores[other, 0] if index else value
        for at, away in enumerate(others_of(count, direct)):
            own[index, at] = held[block_of(count, per, away, 0), :]
            give[index, at] = held[block_of(count, per, away, 1), :]

    for index in range(len(kept) + 1):
        for weight in range(2):
            if index < len(kept):
                first_step(index, weight)
            if index:
                third_step(index - 1, weight)
        if index:
            fourth_step(index - 1)


def others_of(count, direct):
    return [away for away in range(count // 2) if away != direct]


def stat(kept, direct, limit, cost, count, drift, series, weights):
    points = series.shape[0] * BLK // 2
    rows = math.isqrt(points)
    per = points // BLK // count
    chips = count // 2
    pairs = tuple(sorted({pair for pair, _ in kept}))
    inputs = (drift, series, weights, dft_table(rows), twist_table(rows), chirp_table(rows, pairs))
    hbm = pl.BlockSpec(memory_space=pltpu.HBM)
    shapes = [(len(kept), chips - 1, per, BLK)] * 2 + [(2, len(kept), per, BLK)]
    return pl.pallas_call(
        functools.partial(stat_kernel, kept, direct, count),
        out_shape=tuple(jax.ShapeDtypeStruct(shape, F32) for shape in shapes),
        in_specs=[hbm] * 6,
        out_specs=(pl.BlockSpec(memory_space=pltpu.VMEM),) * 3,
        scratch_shapes=[
            pltpu.VMEM(series.shape, BF16),
            pltpu.VMEM(weights.shape, F32),
            pltpu.VMEM((2 * rows, 2 * rows), BF16),
            pltpu.VMEM((2, rows, rows), F32),
            pltpu.VMEM((len(pairs), 2, rows, rows), F32),
            pltpu.VMEM(series.shape, F32),
            pltpu.VMEM((4, rows, rows), F32),
            pltpu.SMEM((3,), F32),
            pltpu.VMEM((MOVED, points // BLK + 2 * PAD, BLK), F32),
            pltpu.SMEM(drift.shape, jnp.int32),
            pltpu.SemaphoreType.DMA((6,)),
        ],
        compiler_params=pltpu.CompilerParams(vmem_limit_bytes=int(limit * 2**20)),
        cost_estimate=pl.CostEstimate(flops=cost, bytes_accessed=3 * 2**20, transcendentals=0),
    )(*[pltpu.with_memory_space_constraint(array, pltpu.HBM) for array in inputs])


def sum_kernel(plan, segments, has_start, tracks, meta, *refs):
    start = refs[0] if has_start else None
    blocks, (out, gathered, total, sems) = refs[has_start:-4], refs[-4:]
    total_rows = gathered.shape[0]
    width = gathered.shape[1]
    me = lax.axis_index("seg")
    core, chip = lax.rem(me, 2), lax.div(me, 2)
    level, other, away = meta[0:1], meta[1:2], meta[2:3]
    segment = 2 * lax.bitwise_xor(away, chip) + lax.bitwise_xor(other, core)
    places = lax.broadcasted_iota(jnp.int32, (segments, total_rows), 0)
    chosen = (places == segment).astype(F32).astype(BF16)
    named = jnp.dot(
        tracks[...].astype(F32).astype(BF16), chosen, preferred_element_type=F32
    )
    pick = jnp.where((named == level.astype(F32)) | (level < 0), 1.0, 0.0).astype(BF16)
    per = width // BLK
    size = min(CHUNK, width)
    leave = []
    for column in range(0, width, size):
        here = slice(column, column + size)
        for tile in range(column // BLK, (column + size) // BLK):
            at = 0
            for block, height in zip(blocks, plan):
                gathered[at : at + height, tile * BLK : (tile + 1) * BLK] = block[
                    pl.ds(tile, height, stride=per), :
                ]
                at += height
        value = gathered[:, here]
        high = value.astype(BF16)
        low = (value - high.astype(F32)).astype(BF16)
        result = jnp.dot(pick, high, preferred_element_type=F32)
        result = result + jnp.dot(pick, low, preferred_element_type=F32)
        result = result * (1.0 / segments)
        if has_start:
            total[:, here] = result + start[:, here]
            leave.append(
                pltpu.make_async_copy(
                    total.at[:, here], out.at[:, here], sems.at[column // size]
                )
            )
            leave[-1].start()
        else:
            out[:, here] = result
    for move in leave:
        move.wait()


def track_sum(tracks, parts, start=None):
    ntrack, segments = tracks.shape
    plan = [len(levels) for _, levels in parts]
    width = parts[0][0].shape[0] * BLK // plan[0]
    meta = np.array([row for _, levels in parts for row in levels]).T
    starts = [] if start is None else [start]
    held = (ntrack, width) if starts else (8, BLK)
    place = pltpu.HBM if starts else pltpu.VMEM
    return pl.pallas_call(
        functools.partial(sum_kernel, plan, segments, len(starts)),
        out_shape=jax.ShapeDtypeStruct((ntrack, width), F32),
        out_specs=pl.BlockSpec(memory_space=place),
        scratch_shapes=[
            pltpu.VMEM((sum(plan), width), F32),
            pltpu.VMEM(held, F32),
            pltpu.SemaphoreType.DMA((max(1, width // CHUNK),)),
        ],
        compiler_params=pltpu.CompilerParams(vmem_limit_bytes=32 * 2**20),
    )(tracks, jnp.asarray(meta, jnp.int32), *starts, *[block for block, _ in parts])


def local(count, strain_series, antenna, drift, tracks):
    points = strain_series.shape[2]
    tile = lambda array: array.reshape(2, points // BLK, BLK).transpose(1, 0, 2).reshape(-1, BLK)
    series, weights = tile(strain_series), tile(antenna)
    chips = count // 2
    half = chips // 2
    even_first = lambda away: (away % 2, away)
    far, near = sorted(range(half, chips), key=even_first), sorted(range(1, half), key=even_first)
    order = [0] + far[:1] + near[:1] + far[1:] + near[:0:-1]
    early = order[: 1 + half - half // 4]
    early += [away for away in near[-1:] if away not in early]
    swap = lambda hop: [(device, device ^ hop) for device in range(count)]
    send = lambda array, hop: lax.ppermute(array, "seg", swap(hop)) if hop else array
    pack = lambda rows: jnp.stack(rows).reshape(-1, BLK)

    direct = order[1]
    own, give, both_cores = stat(EARLY, direct, 32, 10**9, count, drift, series, weights)
    straight = send(both_cores, 2 * direct)
    got = send(give, 1)
    rows, names = [own[0] + got[0]], [(-1, 0)]
    for index, (pair, side) in enumerate(EARLY[1:]):
        for other, part in enumerate((own, got)):
            rows.append(part[1 + index] - part[0])
            names.append((level_of(pair, side), other))
    place = {away: at for at, away in enumerate(others_of(count, direct))}
    parts = {}
    for away in order:
        if away == direct:
            continue
        block = send(pack([row[place[away]] for row in rows]), 2 * away)
        parts[away] = [(block, [(level, other, away) for level, other in names])]
    straight, _ = lax.optimization_barrier((straight, parts[near[-1]][0][0] if near else straight))
    levels = [-1] + [level_of(pair, side) for pair, side in EARLY[1:]]
    parts[direct] = [
        (block.reshape(-1, BLK), [(level, other, direct) for level in levels])
        for other, block in enumerate((straight[0], send(straight[1], 1)))
    ]
    first = [part for away in early for part in parts[away]]
    last = [part for away in order if away not in early for part in parts[away]]
    return track_sum(tracks, last, track_sum(tracks, first))


def solution(mesh):
    return jax.shard_map(
        functools.partial(local, mesh.shape["seg"]),
        mesh=mesh,
        in_specs=(
            P(("sky", "seg"), None, None),
            P(("sky", "seg"), None, None),
            P(("sky", "seg"), None),
            P(),
        ),
        out_specs=P("sky", "seg"),
        check_vma=False,
    )
```
